128 devices in a mesh: attn: 8 (over y, core), ffn: 16 (over x, z).
Axes of the slice: x: 4, y: 4, z: 4, core: 2. Of those that a mesh axis runs over, the one named last changes fastest.
Arguments:
- query_latent: bfloat16 [768, 64, 512], P('attn', 'ffn'), may hold values from -72 to 72
- query_rope: bfloat16 [768, 64, 64], P('attn', 'ffn'), may hold values from -6 to 6
- cache_latent: bfloat16 [768, 64, 512], P('attn'), may hold values from -6 to 6
- cache_rope: bfloat16 [768, 64, 64], P('attn'), may hold values from -6 to 6
- lengths: int32 [768], P('attn'), may hold values from 1 to 64, 16384 in all
- value_up: bfloat16 [64, 512, 128], P('ffn'), may hold values from -0.25 to 0.25
- out_proj: bfloat16 [64, 128, 7168], P('ffn'), may hold values from -0.0625 to 0.0625
- residual: bfloat16 [768, 7168], P(('attn', 'ffn')), may hold values from -6 to 6
- norm_gain: bfloat16 [7168], replicated, may hold values from 0.099609375 to 1.8984375
- expert_ids: int32 [768, 8], P(('attn', 'ffn')), may hold values from 0 to 15, all different within a row; in each aligned block of 6 rows (0 to 5, 6 to 11, ...) at most 4 rows name the same one
- route_weights: float32 [768, 8], P(('attn', 'ffn')), may hold values from 0.1 to 0.6
- gate_proj: bfloat16 [16, 7168, 2048], P('ffn', None, 'attn'), may hold values from -0.0625 to 0.0625
- up_proj: bfloat16 [16, 7168, 2048], P('ffn', None, 'attn'), may hold values from -0.0625 to 0.0625
- down_proj: bfloat16 [16, 2048, 7168], P('ffn', 'attn'), may hold values from -0.125 to 0.125
Outputs:
- layer_out: bfloat16 [768, 7168], P(('attn', 'ffn'))
The draws below stay inside these ranges and needn't reach their ends.
Inputs may be any that keep to these rules, and one draw needn't show every extreme that they name: `expert_ids`: each row names 8 different experts; among the rows of one device (aligned blocks of 6 rows) no expert is named by more than 4 rows, and in some block one expert is named by exactly 4. `lengths`: the largest length is exactly 64.
All inputs are finite; a program needn't handle non-finite values. No bound on the sum of `lengths` on one device may be relied on, other than what follows from the above.
Results may differ from the reference program's by a relative error of at most 0.02.
Values may be sent and summed in bfloat16 or wider, within the bound.
No kernel may reach another device: no remote copies, remote signals or barrier semaphores. Data moves between devices by JAX's collectives and lax.ppermute only.
A program may use at most 128 MiB of HBM per device.

```python
import math
import jax
import jax.numpy as jnp
import numpy as np
from jax import lax

D = 7168
LATENT = 512
ROPE = 64
VDIM = 128
HEADS = 64
FFH = 2048
TOPK = 8
LMAX = 64
EXPERTS = 16
ROWS = 768
RL = 6
CAP = 4


def shared_latent(key):
    return jnp.clip(jax.random.normal(key, (ROWS, LMAX, LATENT), jnp.float32), -6.0, 6.0)


def draw_cache_latent(key, part):
    latent = shared_latent(key)
    return latent.astype(jnp.bfloat16)


def draw_query_latent(key, part):
    key = jax.random.fold_in(key, 12)
    fresh = jnp.clip(jax.random.normal(key, (ROWS, HEADS, LATENT), jnp.float32), -6.0, 6.0)
    return fresh.astype(jnp.bfloat16)


def level_of(rng, extent, split, least, top_value):
    def one(axis_at, shards_of):
        heights = jax.random.uniform(jax.random.fold_in(jax.random.fold_in(rng, 6), axis_at), (shards_of,), jnp.float32, least / len(split), top_value / len(split))
        return jnp.repeat(jnp.exp(heights), extent[axis_at] // shards_of).reshape((-1,) + (1,) * (len(extent) - axis_at - 1))

    factor_of = one(*split[0])
    for cut in split[1:]:
        factor_of = factor_of * one(*cut)
    return factor_of


def profile(count, total, bound, skew):
    portions = [(1 << 20) // math.isqrt(standing ** skew) + 1 for standing in range(2, count + 1)]
    spare, holding = total - bound - (count - 1), [1] * (count - 1)
    while spare > 0:
        movable = [i for i in range(count - 1) if holding[i] < bound]
        whole, left = sum([portions[i] for i in movable]), spare
        for i in movable:
            extra = min(bound - holding[i], max(1, left * portions[i] // whole), spare)
            holding[i] = holding[i] + extra
            spare = spare - extra
    return np.array([bound] + holding)


def uneven(key, amount, total, reach, skew):
    if amount == 2:
        one = jax.random.randint(key, (), max(1, total - reach), min(reach, total - 1) + 1)
        return jnp.stack([one, total - one])
    sizes = jnp.asarray(profile(amount, total, reach, skew), jnp.int32)
    couples = (amount - 1) // 2
    source_of, sink = sizes[1:1 + 2 * couples:2], sizes[2:2 + 2 * couples:2]
    slack = jnp.minimum(source_of - 1, reach - sink)
    passed = jax.random.randint(jax.random.fold_in(key, 1), (couples,), 0, 1 << 20) % (slack + 1)
    sizes = sizes.at[1:1 + 2 * couples:2].set(source_of - passed).at[2:2 + 2 * couples:2].set(sink + passed)
    return sizes[jax.random.permutation(jax.random.fold_in(key, 2), amount)]


def routed_block(rng, own, number, rows, count, top, reach, slope):
    sequence = jax.random.permutation(rng, count)
    crowded, usual = portions_of(count, rows * top, reach, slope, True), portions_of(count, rows * top, reach, slope, False)
    places = jnp.arange(count)

    def named(sizes, turn):
        used = int((sizes > 0).sum())
        fixed = max(1, used // 4)
        moved = fixed + (places - fixed + turn * (used - fixed)) % max(1, count - fixed)
        return jnp.zeros((count,), jnp.int32).at[sequence[jnp.where(places < fixed, places, moved)]].set(jnp.asarray(sizes, jnp.int32))

    sizes = jnp.where(number % 4 == 0, named(crowded, number // 4), named(usual, number - number // 4 - 1))
    mixed = jax.random.permutation(jax.random.fold_in(own, 3), count)
    donor, taker = mixed[0:count // 2 * 2:2], mixed[1:count // 2 * 2:2]
    room = jnp.minimum(sizes[donor] - 1, reach - sizes[taker]) // 2
    room = jnp.where((donor == sequence[0]) | (taker == sequence[0]) | (sizes[taker] == 0), 0, jnp.maximum(room, 0))
    moved = jax.random.randint(jax.random.fold_in(own, 4), (count // 2,), 0, 1 << 20) % (room + 1)
    sizes = sizes.at[donor].add(-moved).at[taker].add(moved)
    members = jnp.searchsorted(jnp.cumsum(sizes), jnp.arange(rows * top), side="right").astype(jnp.int32)
    table = members.reshape(top, rows).T
    table = table[jax.random.permutation(jax.random.fold_in(own, 1), rows)]
    turn = jax.random.randint(jax.random.fold_in(own, 2), (rows, 1), 0, top)
    return jnp.take_along_axis(table, (jnp.arange(top)[None, :] + turn) % top, axis=1)


def portions_of(count, total, limit, lean, full):
    weights = [(1 << 20) // math.isqrt(rank ** lean) + 1 for rank in range(1, count + 1)]
    largest = limit if full else min(limit, max(-(-total // count), total * weights[0] // sum(weights)))
    least = 1 if total - largest >= count - 1 else 0
    given, rest = [largest] + [least] * (count - 1), total - largest - least * (count - 1)
    while rest > 0:
        candidates = [i for i in range(1, count) if given[i] < largest] or [i for i in range(1, count) if given[i] < limit]
        whole, remaining = sum([weights[i] for i in candidates]), rest
        for i in candidates:
            more = min(limit - given[i], max(1, remaining * weights[i] // whole), rest)
            given[i] = given[i] + more
            rest = rest - more
    return np.array(given)


def bell_draw(rng, extent, deviation, bound, pieces=(), held_as=jnp.bfloat16):
    loudness = level_of(rng, extent, pieces, -0.22, 0.18) if pieces else 1.0
    values = jax.random.normal(rng, extent, jnp.float32) * deviation * loudness
    return jnp.minimum(jnp.maximum(values, -bound), bound).astype(held_as)


def setup_inputs(seed: int = 0) -> dict:
    splits = jax.random.split(jax.random.key(seed), 15)
    query_latent = draw_query_latent(jax.random.fold_in(splits[14], 71), 0)
    query_rope = bell_draw(splits[1], (ROWS, HEADS, ROPE), 1.0, 6.0, ((0, 8), (1, 16)))
    cache_latent = draw_cache_latent(jax.random.fold_in(splits[14], 71), 0)
    cache_rope = bell_draw(splits[3], (ROWS, LMAX, ROPE), 1.0, 6.0, ((0, 8),))
    lengths = uneven(splits[4], ROWS, ROWS * LMAX // 3, LMAX, 2).astype(jnp.int32)
    value_up = bell_draw(splits[5], (HEADS, LATENT, VDIM), LATENT ** -0.5, 0.25, ((0, 16),))
    out_proj = bell_draw(splits[6], (HEADS, VDIM, D), (HEADS * VDIM) ** -0.5, 0.0625, ((0, 16),))
    residual = bell_draw(splits[7], (ROWS, D), 1.0, 6.0, ((0, 128),))
    norm_gain = jnp.clip(1.0 + 0.18 * jax.random.normal(splits[8], (D,), jnp.float32), 0.099609375, 1.8984375).astype(jnp.bfloat16)
    expert_ids_keys = jax.random.split(jax.random.fold_in(splits[9], 1), ROWS // RL)
    expert_ids_turns = jax.random.permutation(jax.random.fold_in(splits[9], 3), ROWS // RL)
    expert_ids = jax.vmap(lambda own, number: routed_block(jax.random.fold_in(splits[9], 2), own, number, RL, EXPERTS, TOPK, CAP, 2))(expert_ids_keys, expert_ids_turns).reshape((ROWS, TOPK))
    route_weights = jnp.clip(0.1 + 0.5 * jax.random.uniform(splits[10], (ROWS, TOPK), jnp.float32) ** level_of(splits[10], (ROWS, TOPK), ((0, 128),), -0.2, 0.2), 0.1, 0.6)
    gate_proj = bell_draw(splits[11], (EXPERTS, D, FFH), D ** -0.5, 0.0625, ((0, 16), (2, 8)))
    up_proj = bell_draw(splits[12], (EXPERTS, D, FFH), D ** -0.5, 0.0625, ((0, 16), (2, 8)))
    down_proj = bell_draw(splits[13], (EXPERTS, FFH, D), FFH ** -0.5, 0.125, ((0, 16), (1, 8)))
    return {"query_latent": query_latent, "query_rope": query_rope, "cache_latent": cache_latent, "cache_rope": cache_rope, "lengths": lengths, "value_up": value_up, "out_proj": out_proj, "residual": residual, "norm_gain": norm_gain, "expert_ids": expert_ids, "route_weights": route_weights, "gate_proj": gate_proj, "up_proj": up_proj, "down_proj": down_proj}


def reference(query_latent, query_rope, cache_latent, cache_rope, lengths, value_up, out_proj, residual, norm_gain, expert_ids, route_weights, gate_proj, up_proj, down_proj):
    score_scale = (VDIM + ROPE) ** (-0.5)
    cache_f = cache_latent.astype(jnp.float32)
    scores = jnp.einsum('rhc,rlc->rhl', query_latent.astype(jnp.float32), cache_f)
    scores = scores + jnp.einsum('rhc,rlc->rhl', query_rope.astype(jnp.float32), cache_rope.astype(jnp.float32))
    scores = scores * score_scale
    live = jnp.arange(LMAX, dtype=jnp.int32)[None, None, :] < lengths[:, None, None]
    scores = jnp.where(live, scores, jnp.float32(-1e+30))
    top_score = lax.optimization_barrier(jnp.max(scores, axis=2, keepdims=True))
    expo = jnp.where(live, jnp.exp(scores - top_score), jnp.float32(0.0))
    probs = (expo / lax.optimization_barrier(jnp.sum(expo, axis=2, keepdims=True))).astype(jnp.bfloat16)
    head_latent = jnp.einsum('rhl,rlc->rhc', probs.astype(jnp.float32), cache_f).astype(jnp.bfloat16)
    head_values = jnp.einsum('rhc,hcv->rhv', head_latent.astype(jnp.float32), value_up.astype(jnp.float32)).astype(jnp.bfloat16)
    attended = jnp.einsum('rhv,hvd->rd', head_values.astype(jnp.float32), out_proj.astype(jnp.float32))
    mixed_in = residual.astype(jnp.float32) + attended
    inverse = lax.rsqrt(lax.optimization_barrier(jnp.mean(mixed_in * mixed_in, axis=1, keepdims=True)) + 1e-06)
    normed = (mixed_in * inverse * norm_gain.astype(jnp.float32)[None, :]).astype(jnp.bfloat16)
    most_rows = min(ROWS, ROWS // RL * CAP)

    def one_expert(total, expert):
        named = expert_ids == expert
        weight_row = lax.optimization_barrier(jnp.sum(jnp.where(named, route_weights, jnp.float32(0.0)), axis=1))
        routed = jnp.any(named, axis=1)
        order = jnp.argsort(jnp.where(routed, 0, 1).astype(jnp.int32), stable=True)[:most_rows].astype(jnp.int32)
        picked = normed[order]
        gate = jnp.dot(picked, gate_proj[expert], preferred_element_type=jnp.float32)
        upper = jnp.dot(picked, up_proj[expert], preferred_element_type=jnp.float32)
        hidden = (jax.nn.silu(gate) * upper).astype(jnp.bfloat16)
        expert_out = jnp.dot(hidden, down_proj[expert], preferred_element_type=jnp.float32).astype(jnp.bfloat16)
        added = weight_row[order][:, None] * expert_out.astype(jnp.float32)
        return (total.at[order].add(added), None)
    routed_sum, unused = lax.scan(one_expert, jnp.zeros((ROWS, D), jnp.float32), jnp.arange(EXPERTS, dtype=jnp.int32))
    return (mixed_in + routed_sum).astype(jnp.bfloat16)
```

```python
import jax
import jax.numpy as jnp
from jax import lax
from jax.sharding import PartitionSpec as P


def local(
    query_latent,
    query_rope,
    cache_latent,
    cache_rope,
    lengths,
    value_up,
    out_proj,
    residual,
    norm_gain,
    expert_ids,
    route_weights,
    gate_proj,
    up_proj,
    down_proj,
):
    score_scale = (value_up.shape[2] + query_rope.shape[2]) ** (-0.5)
    cache_length = cache_latent.shape[1]
    row_count = residual.shape[0]
    scores = jnp.einsum(
        "rhc,rlc->rhl", query_latent, cache_latent, preferred_element_type=jnp.float32
    )
    scores = scores + jnp.einsum(
        "rhc,rlc->rhl", query_rope, cache_rope, preferred_element_type=jnp.float32
    )
    scores = scores * score_scale
    live = jnp.arange(cache_length, dtype=jnp.int32)[None, None, :] < lengths[:, None, None]
    scores = jnp.where(live, scores, jnp.float32(-1e30))
    top_score = jnp.max(scores, axis=2, keepdims=True)
    expo = jnp.where(live, jnp.exp(scores - top_score), jnp.float32(0.0))
    probs = (expo / jnp.sum(expo, axis=2, keepdims=True)).astype(jnp.bfloat16)
    head_latent = jnp.einsum(
        "rhl,rlc->rhc", probs, cache_latent, preferred_element_type=jnp.float32
    ).astype(jnp.bfloat16)
    head_values = jnp.einsum(
        "rhc,hcv->rhv", head_latent, value_up, preferred_element_type=jnp.float32
    ).astype(jnp.bfloat16)
    owners = lax.axis_size("ffn")
    width = residual.shape[1]
    parts = 4
    projected = jnp.einsum(
        "rhv,hvd->rd", head_values, out_proj, preferred_element_type=jnp.float32
    ).astype(jnp.bfloat16)
    pieces = (
        projected.reshape(owners, row_count, parts, width // parts)
        .transpose(0, 2, 1, 3)
        .reshape(owners, parts * row_count, width // parts)
    )
    pieces = lax.all_to_all(pieces, "ffn", split_axis=0, concat_axis=0, tiled=True)
    attended = (
        jnp.sum(pieces.astype(jnp.float32), axis=0)
        .reshape(parts, row_count, width // parts)
        .transpose(1, 0, 2)
        .reshape(row_count, width)
    )
    mixed_in = residual.astype(jnp.float32) + attended
    inverse = lax.rsqrt(jnp.mean(mixed_in * mixed_in, axis=1, keepdims=True) + 1e-06)
    normed = (mixed_in * inverse * norm_gain.astype(jnp.float32)[None, :]).astype(jnp.bfloat16)
    top_count = expert_ids.shape[1]
    capacity = min(row_count, row_count * top_count // owners + 1)
    expert_range = jnp.arange(owners, dtype=jnp.int32)
    named = expert_ids[:, :, None] == expert_range[None, None, :]
    routed = jnp.sum(named.astype(jnp.int32), axis=1)
    weight_table = jnp.sum(jnp.where(named, route_weights[:, :, None], jnp.float32(0.0)), axis=1)
    slot_rank = jnp.cumsum(routed, axis=0) - routed
    slot_range = jnp.arange(capacity, dtype=jnp.int32)
    placed = (routed.T[:, None, :] == 1) & (slot_rank.T[:, None, :] == slot_range[None, :, None])
    outgoing = jnp.einsum(
        "ecr,rd->ecd", placed.astype(jnp.bfloat16), normed, preferred_element_type=jnp.float32
    ).astype(jnp.bfloat16)
    arrived = lax.all_to_all(outgoing, "ffn", split_axis=0, concat_axis=0, tiled=True)
    flat_rows = arrived.reshape(owners * capacity, width)
    block_rows = lax.all_gather(flat_rows, "attn", axis=0, tiled=True)
    gate = jnp.dot(block_rows, gate_proj[0], preferred_element_type=jnp.float32)
    upper = jnp.dot(block_rows, up_proj[0], preferred_element_type=jnp.float32)
    hidden = (jax.nn.silu(gate) * upper).astype(jnp.bfloat16)
    partial_value = jnp.dot(hidden, down_proj[0], preferred_element_type=jnp.float32)
    summed = lax.psum_scatter(
        partial_value.astype(jnp.bfloat16), "attn", scatter_dimension=0, tiled=True
    )
    returned = lax.all_to_all(
        summed.reshape(owners, capacity, width), "ffn", split_axis=0, concat_axis=0, tiled=True
    )
    weighting = placed.astype(jnp.float32) * weight_table.T[:, None, :]
    routed_sum = jnp.einsum(
        "ecr,ecd->rd", weighting, returned.astype(jnp.float32), precision=lax.Precision.HIGHEST
    )
    return (mixed_in + routed_sum).astype(jnp.bfloat16)


def solution(mesh):
    return jax.shard_map(
        local,
        mesh=mesh,
        in_specs=(
            P("attn", "ffn", None),
            P("attn", "ffn", None),
            P("attn", None, None),
            P("attn", None, None),
            P("attn"),
            P("ffn", None, None),
            P("ffn", None, None),
            P(("attn", "ffn"), None),
            P(),
            P(("attn", "ffn"), None),
            P(("attn", "ffn"), None),
            P("ffn", None, "attn"),
            P("ffn", None, "attn"),
            P("ffn", "attn", None),
        ),
        out_specs=P(("attn", "ffn"), None),
        check_vma=False,
    )
```

```python
import jax
import jax.numpy as jnp
from jax import lax
from jax.experimental import pallas as pl
from jax.experimental.pallas import tpu as pltpu
from jax.sharding import PartitionSpec as P

PARTS = 4
UNIT = 512
IN_RING = 9 * UNIT
OUT_RING = 10 * UNIT
F32 = jnp.float32
BF16 = jnp.bfloat16


def dot(a, b):
    return jnp.dot(a, b, preferred_element_type=F32)


def order_matrix(plane, planes, owners, capacity, dtype):
    count = planes * owners * capacity
    out = lax.broadcasted_iota(jnp.int32, (count, count), 0)
    at = lax.broadcasted_iota(jnp.int32, (count, count), 1)
    y, f, c = out // (owners * capacity), (out // capacity) % owners, out % capacity
    source = (f * planes + (y - plane + planes) % planes) * capacity + c
    return (source == at).astype(dtype)


def rest_kernel(dims, place, order, mine, other, gate, upper, out, total):
    step = pl.program_id(0)
    planes, rows = dims

    @pl.when(step == 0)
    def _():
        total[...] = jnp.zeros_like(total)

    both = jnp.concatenate([gate[0], upper[0]], axis=1)
    for at, ref in enumerate((mine, other)):
        ordered = dot(order[...], ref[...]).astype(BF16)
        total[at] += dot(ordered, both)

    @pl.when(step == pl.num_programs(0) - 1)
    def _():
        for at in range(2):
            core = place[0] if at == 0 else 1 - place[0]
            for y in range(planes):
                out[y, core] = total[at, y * rows : (y + 1) * rows]


def gate_rest(place, order, mine, other, gate_proj, up_proj, start, tile=UNIT):
    count, depth = mine.shape
    hidden = gate_proj.shape[2]
    planes = 4
    weight = pl.BlockSpec((1, tile, hidden), lambda k, p: (0, start // tile + k, 0))
    rows = pl.BlockSpec((count, tile), lambda k, p: (0, k))
    shape = (planes, 2, count // planes, 2 * hidden)
    return pl.pallas_call(
        lambda *refs: rest_kernel((planes, count // planes), *refs),
        out_shape=jax.ShapeDtypeStruct(shape, F32),
        grid_spec=pltpu.PrefetchScalarGridSpec(
            num_scalar_prefetch=1,
            grid=(depth // tile,),
            in_specs=[pl.BlockSpec((count, count), lambda k, p: (0, 0)), rows, rows, weight, weight],
            out_specs=pl.BlockSpec(shape, lambda k, p: (0, 0, 0, 0)),
            scratch_shapes=[pltpu.VMEM((2, count, 2 * hidden), F32)],
        ),
        compiler_params=pltpu.CompilerParams(vmem_limit_bytes=60 << 20),
        cost_estimate=pl.CostEstimate(
            flops=4 * count * depth * (count + 2 * hidden),
            bytes_accessed=4 * count * depth + 4 * depth * hidden,
            transcendentals=0,
        ),
    )(place, order, mine, other, gate_proj, up_proj)


def ring_kernel(rows, gate, upper, rest, out, total):
    step = pl.program_id(0)
    hidden = out.shape[1]

    @pl.when(step == 0)
    def _():
        total[...] = rest[...]

    both = jnp.concatenate([gate[0], upper[0]], axis=1)
    total[...] += dot(rows[...], both)

    @pl.when(step == pl.num_programs(0) - 1)
    def _():
        gated = total[:, :hidden]
        out[...] = (gated * jax.nn.sigmoid(gated) * total[:, hidden:]).astype(out.dtype)


def gate_ring(rows, gate_proj, up_proj, rest, tile=UNIT):
    count, depth = rows.shape
    hidden = gate_proj.shape[2]
    weight = pl.BlockSpec((1, tile, hidden), lambda k: (0, k, 0))
    whole = pl.BlockSpec((count, 2 * hidden), lambda k: (0, 0))
    return pl.pallas_call(
        ring_kernel,
        out_shape=jax.ShapeDtypeStruct((count, hidden), BF16),
        grid=(depth // tile,),
        in_specs=[pl.BlockSpec((count, tile), lambda k: (0, k)), weight, weight, whole],
        out_specs=pl.BlockSpec((count, hidden), lambda k: (0, 0)),
        scratch_shapes=[pltpu.VMEM((count, 2 * hidden), F32)],
        compiler_params=pltpu.CompilerParams(vmem_limit_bytes=60 << 20),
        cost_estimate=pl.CostEstimate(
            flops=4 * count * depth * hidden,
            bytes_accessed=2 * count * depth + 4 * depth * hidden,
            transcendentals=count * hidden,
        ),
    )(rows, gate_proj, up_proj, rest)


def local(
    query_latent,
    query_rope,
    cache_latent,
    cache_rope,
    lengths,
    value_up,
    out_proj,
    residual,
    norm_gain,
    expert_ids,
    route_weights,
    gate_proj,
    up_proj,
    down_proj,
):
    score_scale = (value_up.shape[2] + query_rope.shape[2]) ** (-0.5)
    cache_length = cache_latent.shape[1]
    row_count, width = residual.shape
    owners = lax.axis_size("ffn")
    cores = 2
    planes = lax.axis_size("attn") // cores
    core = lax.axis_index("attn") % cores
    plane = lax.axis_index("attn") // cores
    swap = [(a, a ^ 1) for a in range(planes * cores)]

    def from_plane(v, ahead):
        pairs = [
            (((y + ahead) % planes) * cores + c, y * cores + c)
            for y in range(planes)
            for c in range(cores)
        ]
        return lax.ppermute(v, "attn", pairs)

    def along_planes(v):
        return jnp.stack([v] + [from_plane(v, ahead) for ahead in range(1, planes)])

    named = expert_ids[:, :, None] == jnp.arange(owners, dtype=jnp.int32)[None, None, :]
    table = jnp.concatenate(
        [
            jnp.sum(named.astype(F32), axis=1),
            jnp.sum(jnp.where(named, route_weights[:, :, None], F32(0.0)), axis=1),
        ],
        axis=1,
    )
    tables = along_planes(table)
    capacity = min(row_count, row_count * expert_ids.shape[1] // owners + 1)

    def slots_of(table):
        routed = table[..., :owners]
        weight = table[..., owners:]
        rank = jnp.cumsum(routed, axis=-2) - routed
        routed, weight, rank = (jnp.moveaxis(v, -1, 0)[..., None, :] for v in (routed, weight, rank))
        slot = jnp.arange(capacity, dtype=jnp.int32).astype(F32)[:, None]
        placed = ((routed == 1.0) & (rank == slot)).astype(F32)
        return placed, placed * weight

    placed, weighting = slots_of(table)
    placed_all, weighting_all = slots_of(tables)
    eye = jnp.eye(planes, dtype=F32)

    def block_diagonal(v):
        spread = v[:, :, :, None, :] * eye[None, :, None, :, None]
        return spread.reshape(owners * planes * capacity, planes * row_count)

    placed = placed.reshape(owners * capacity, row_count).astype(BF16)
    weighting = weighting.reshape(owners * capacity, row_count)
    placed_all = block_diagonal(placed_all).astype(BF16)
    weighting_all = block_diagonal(weighting_all)

    scores = jnp.einsum("rhc,rlc->rhl", query_latent, cache_latent, preferred_element_type=F32)
    scores = scores + jnp.einsum("rhc,rlc->rhl", query_rope, cache_rope, preferred_element_type=F32)
    scores = scores * score_scale
    live = jnp.arange(cache_length, dtype=jnp.int32)[None, None, :] < lengths[:, None, None]
    scores = jnp.where(live, scores, F32(-1e30))
    top_score = jnp.max(scores, axis=2, keepdims=True)
    expo = jnp.where(live, jnp.exp(scores - top_score), F32(0.0))
    probs = (expo / jnp.sum(expo, axis=2, keepdims=True)).astype(BF16)
    head_latent = jnp.einsum(
        "rhl,rlc->rhc", probs, cache_latent, preferred_element_type=F32
    ).astype(BF16)
    head_values = jnp.einsum(
        "rhc,hcv->rhv", head_latent, value_up, preferred_element_type=F32
    ).astype(BF16)

    projected = jnp.einsum(
        "rhv,hvd->rd", head_values, out_proj, preferred_element_type=F32
    ).astype(BF16)
    pieces = (
        projected.reshape(owners, row_count, PARTS, width // PARTS)
        .transpose(0, 2, 1, 3)
        .reshape(owners, PARTS * row_count, width // PARTS)
    )
    pieces = lax.all_to_all(pieces, "ffn", split_axis=0, concat_axis=0, tiled=True)
    attended = (
        jnp.sum(pieces.astype(F32), axis=0)
        .reshape(PARTS, row_count, width // PARTS)
        .transpose(1, 0, 2)
        .reshape(row_count, width)
    )
    mixed = residual.astype(F32) + attended
    inverse = lax.rsqrt(jnp.mean(mixed * mixed, axis=1, keepdims=True) + 1e-06)
    normed = (mixed * inverse * norm_gain.astype(F32)[None, :]).astype(BF16)

    outgoing = dot(placed, normed[:, :IN_RING]).astype(BF16).reshape(owners, capacity, IN_RING)
    arrived = lax.all_to_all(outgoing, "ffn", split_axis=0, concat_axis=0, tiled=True)
    arrived = arrived.reshape(owners * capacity, IN_RING)

    rest = width - IN_RING
    near = along_planes(normed[:, IN_RING:]).reshape(planes * row_count, rest)
    near, arrived = lax.optimization_barrier((near, arrived))
    ring_rows = lax.all_gather(arrived, "attn", axis=0, tiled=True)
    outgoing = dot(placed_all, near).astype(BF16).reshape(owners, planes * capacity, rest)
    mine = lax.all_to_all(outgoing, "ffn", split_axis=0, concat_axis=0, tiled=True)
    mine = mine.reshape(owners * planes * capacity, rest)
    other = lax.ppermute(mine, "attn", swap)
    order = order_matrix(plane, planes, owners, capacity, BF16)
    hidden_count = gate_proj.shape[2]
    sums = gate_rest(core.reshape(1), order, mine, other, gate_proj, up_proj, IN_RING)
    sums = sums.reshape(planes * cores * owners * capacity, 2 * hidden_count)
    hidden = gate_ring(ring_rows, gate_proj, up_proj, sums)

    partial_value = dot(hidden, down_proj[0, :, :OUT_RING]).astype(BF16)
    hidden, partial_value = lax.optimization_barrier((hidden, partial_value))
    summed = lax.psum_scatter(partial_value, "attn", scatter_dimension=0, tiled=True)

    by_core = hidden.reshape(planes, cores, owners * capacity, hidden_count)

    def share(core):
        rows = lax.dynamic_index_in_dim(by_core, core, 1, False)
        rows = rows.reshape(planes * owners * capacity, hidden_count)
        rows = dot(order.T, rows).astype(BF16)
        return dot(rows, down_proj[0, :, OUT_RING:])

    rest = width - OUT_RING
    theirs = lax.ppermute(share(1 - core).astype(BF16), "attn", swap)
    ours = (share(core) + theirs.astype(F32)).astype(BF16)
    ours = ours.reshape(owners, planes * capacity, rest)
    ours = lax.all_to_all(ours, "ffn", split_axis=0, concat_axis=0, tiled=True)
    ours = jnp.einsum(
        "sr,sd->rd",
        weighting_all,
        ours.reshape(owners * planes * capacity, rest).astype(F32),
        precision=lax.Precision.HIGHEST,
    ).astype(BF16)
    ours = ours.reshape(planes, row_count, rest)
    sum_rest = ours[0].astype(F32)
    for ahead in range(1, planes):
        sum_rest = sum_rest + from_plane(ours[planes - ahead], ahead).astype(F32)

    returned = lax.all_to_all(
        summed.reshape(owners, capacity, OUT_RING), "ffn", split_axis=0, concat_axis=0, tiled=True
    )
    sum_ring = jnp.einsum(
        "sr,sd->rd",
        weighting,
        returned.reshape(owners * capacity, OUT_RING).astype(F32),
        precision=lax.Precision.HIGHEST,
    )
    return (mixed + jnp.concatenate([sum_ring, sum_rest], axis=1)).astype(BF16)


def solution(mesh):
    return jax.shard_map(
        local,
        mesh=mesh,
        in_specs=(
            P("attn", "ffn", None),
            P("attn", "ffn", None),
            P("attn", None, None),
            P("attn", None, None),
            P("attn"),
            P("ffn", None, None),
            P("ffn", None, None),
            P(("attn", "ffn"), None),
            P(),
            P(("attn", "ffn"), None),
            P(("attn", "ffn"), None),
            P("ffn", None, "attn"),
            P("ffn", None, "attn"),
            P("ffn", "attn", None),
        ),
        out_specs=P(("attn", "ffn"), None),
        check_vma=False,
    )
```

```python
import math

import jax
import jax.numpy as jnp
from jax import lax
from jax.experimental import pallas as pl
from jax.experimental.pallas import tpu as pltpu
from jax.sharding import PartitionSpec as P

PARTS = 4
UNIT = 512
IN_RING = 4352
OUT_RING = 4352
F32 = jnp.float32
BF16 = jnp.bfloat16


def dot(a, b):
    return jnp.dot(a, b, preferred_element_type=F32)


GROUP = 4

def attend_kernel(
    scale,
    owners,
    parts,
    lengths,
    query,
    cache,
    query_rope,
    cache_rope,
    value_up,
    out_proj,
    out,
    rope,
    latent,
    values,
    weights,
    arrived,
):
    step = pl.program_id(0)
    heads = query.shape[1]
    depth, positions = cache.shape[2], cache.shape[1]
    rows = cache.shape[0]
    count = GROUP * heads
    width = weights.shape[1] // parts
    fetches = [
        pltpu.make_async_copy(
            out_proj.at[:, pl.ds(part * width, width)],
            weights.at[:, pl.ds(part * width, width)],
            arrived.at[part],
        )
        for part in range(parts)
    ]

    @pl.when(step == 0)
    def _():
        for fetch in fetches:
            fetch.start()
        for h in range(heads):
            vector = query_rope[h].astype(F32)
            parts = []
            for at in range(positions):
                parts.append(jnp.sum(vector * cache_rope[at].astype(F32), axis=0, keepdims=True))
            wide = jnp.concatenate(parts, axis=0).T
            rope[pl.ds(h, wide.shape[0], heads), :] = jnp.concatenate([wide] * 2, axis=1)

    groups = rows // GROUP
    total = rows * heads
    base = pl.multiple_of(step * total, total)
    keys = [
        cache[group * GROUP : (group + 1) * GROUP].reshape(GROUP * positions, depth)
        for group in range(groups)
    ]
    scores = []
    for group in range(groups):
        queries = jnp.concatenate([query[group * GROUP + i] for i in range(GROUP)], axis=0)
        scores.append(
            lax.dot_general(
                queries, keys[group], (((1,), (1,)), ((), ())), preferred_element_type=F32
            )
        )
    scores = jnp.concatenate(scores, axis=0)
    near = rope[pl.ds(base, total), :]
    scores = (scores + jnp.concatenate([near] * (GROUP // 2), axis=1)) * scale
    row = lax.broadcasted_iota(jnp.int32, scores.shape, 0) // heads
    own = lax.broadcasted_iota(jnp.int32, scores.shape, 1) - (row % GROUP) * positions
    limit = jnp.concatenate(
        [jnp.full((heads, GROUP * positions), lengths[step * rows + i], jnp.int32) for i in range(rows)],
        axis=0,
    )
    live = (own >= 0) & (own < limit)
    scores = jnp.where(live, scores, F32(-1e30))
    top = jnp.max(scores, axis=1, keepdims=True)
    expo = jnp.where(live, jnp.exp(scores - top), F32(0.0))
    probs = (expo / jnp.sum(expo, axis=1, keepdims=True)).astype(BF16)
    mixed = jnp.concatenate(
        [
            dot(probs[group * count : (group + 1) * count], keys[group])
            for group in range(groups)
        ],
        axis=0,
    )
    for part in range(depth // 128):
        latent[part, pl.ds(base, total), :] = mixed[:, part * 128 : (part + 1) * 128]

    @pl.when(step == pl.num_programs(0) - 1)
    def _():
        all_rows = values.shape[0]
        size = value_up.shape[2]
        for h in range(heads):
            mixed = jnp.concatenate(
                [latent[part, pl.ds(h, all_rows, heads), :] for part in range(depth // 128)], axis=1
            ).astype(BF16)
            values[:, h * size : (h + 1) * size] = dot(mixed, value_up[h]).astype(BF16)
        own_rows = all_rows // owners
        for part, fetch in enumerate(fetches):
            fetch.wait()
            result = dot(values[...], weights[:, part * width : (part + 1) * width]).astype(BF16)
            for f in range(owners):
                out[f, part * own_rows : (part + 1) * own_rows] = result[
                    f * own_rows : (f + 1) * own_rows
                ]


def attend(
    query, query_rope, cache, cache_rope, lengths, value_up, out_proj, scale, owners, parts, steps=2
):
    rows, heads, depth = query.shape
    positions = cache.shape[1]
    block = rows // steps
    size = heads * value_up.shape[2]
    width = out_proj.shape[2]
    shape = (owners, parts * (rows // owners), width // parts)
    whole = lambda shape: pl.BlockSpec(shape, lambda k, n: (0,) * len(shape))
    query_rope = jnp.transpose(query_rope, (1, 2, 0))
    cache_rope = jnp.transpose(cache_rope, (1, 2, 0))
    return pl.pallas_call(
        lambda *refs: attend_kernel(scale, owners, parts, *refs),
        out_shape=jax.ShapeDtypeStruct(shape, BF16),
        grid_spec=pltpu.PrefetchScalarGridSpec(
            num_scalar_prefetch=1,
            grid=(steps,),
            in_specs=[
                pl.BlockSpec((block, heads, depth), lambda k, n: (k, 0, 0)),
                pl.BlockSpec((block, positions, depth), lambda k, n: (k, 0, 0)),
                whole(query_rope.shape),
                whole(cache_rope.shape),
                whole(value_up.shape),
                pl.BlockSpec(memory_space=pl.ANY),
            ],
            out_specs=whole(shape),
            scratch_shapes=[
                pltpu.VMEM((rows * heads, 2 * positions), F32),
                pltpu.VMEM((depth // 128, rows * heads, 128), F32),
                pltpu.VMEM((rows, size), BF16),
                pltpu.VMEM((size, width), BF16),
                pltpu.SemaphoreType.DMA((parts,)),
            ],
        ),
        compiler_params=pltpu.CompilerParams(vmem_limit_bytes=60 << 20),
        cost_estimate=pl.CostEstimate(
            flops=4 * rows * heads * positions * depth * GROUP + 2 * rows * size * width,
            bytes_accessed=2 * rows * positions * depth + 2 * size * width,
            transcendentals=rows * heads * positions,
        ),
    )(lengths, query, cache, query_rope, cache_rope, value_up, out_proj.reshape(size, width))


OWNED = 4
INNER = 2
SLAB = 1024


def expert_kernel(
    place,
    rows,
    mine,
    other,
    gate_proj,
    up_proj,
    down_proj,
    out,
    theirs,
    ours,
    x,
    x_rest,
    gate_w,
    up_w,
    down_w,
    gate_rest,
    up_rest,
    gate,
    up,
    spread,
    slab,
    share,
    got,
    sent,
):
    core, plane = place[0], place[1]
    depth, rest = x.shape[1], x_rest.shape[1]
    count = mine.shape[0]
    hidden_count = gate_w.shape[1]
    planes, cores, block = gate.shape[:3]
    own = block // OWNED
    tile = depth // INNER
    size = out.shape[1]
    left = down_w.shape[1] - size
    ring_w = [(at * tile, tile) for at in range(INNER)] + [(depth, rest)]

    def fetch(source, target, sem):
        copy = pltpu.make_async_copy(source, target, sem)
        copy.start()
        return copy

    def fetch_weights(at):
        start, length = ring_w[at]
        rows_at = pl.ds(start, length)
        return [
            fetch(gate_proj.at[0, rows_at], gate_w.at[rows_at], got.at[4 * at]),
            fetch(up_proj.at[0, rows_at], up_w.at[rows_at], got.at[4 * at + 1]),
        ]

    waits = {}
    waits[INNER] = fetch_weights(INNER) + [
        fetch(mine, x_rest.at[pl.ds(0, count)], got.at[4 * INNER + 2]),
        fetch(other, x_rest.at[pl.ds(count, count)], got.at[4 * INNER + 3]),
    ]
    for at in range(INNER):
        columns = pl.ds(at * tile, tile)
        waits[at] = fetch_weights(at) + [
            fetch(rows.at[:, columns], x.at[:, columns], got.at[4 * at + 2])
        ]
    down_wait = fetch(down_proj.at[0], down_w, got.at[4 * INNER + 4])

    for copy in waits[INNER]:
        copy.wait()
    gate_rest[...] = dot(x_rest[...], gate_w[depth:])
    up_rest[...] = dot(x_rest[...], up_w[depth:])
    shape = gate.shape
    for at in range(INNER):
        for copy in waits[at]:
            copy.wait()
        start = at * tile
        part = x[:, start : start + tile]
        gate_part = dot(part, gate_w[start : start + tile]).reshape(shape)
        up_part = dot(part, up_w[start : start + tile]).reshape(shape)
        if at == 0:
            gate[...] = gate_part
            up[...] = up_part
        else:
            gate[...] += gate_part
            up[...] += up_part
    for turn in range(planes):
        y = (plane + turn) % planes
        for at in range(cores):
            c = core if at == 0 else 1 - core
            for f in range(own):
                source = slice(
                    at * count + (f * planes + turn) * OWNED,
                    at * count + (f * planes + turn + 1) * OWNED,
                )
                target = slice(f * OWNED, (f + 1) * OWNED)
                gate[y, c, target] += gate_rest[source]
                up[y, c, target] += up_rest[source]
    gated = gate[...]
    hidden = gated * jax.nn.sigmoid(gated) * up[...]
    gate[...] = hidden
    hidden = hidden.reshape(rows.shape[0], hidden_count).astype(BF16)
    for turn in range(planes):
        y = (plane + turn) % planes
        for at in range(cores):
            c = core if at == 0 else 1 - core
            for f in range(own):
                target = slice((f * planes + turn) * OWNED, (f * planes + turn + 1) * OWNED)
                spread[at, target] = gate[y, c, f * OWNED : (f + 1) * OWNED]
    down_wait.wait()
    sends = []
    for at, ref in ((1, theirs), (0, ours)):
        share[at] = dot(spread[at].astype(BF16), down_w[:, size:]).astype(BF16)
        sends.append(fetch(share.at[at], ref, sent.at[at]))
    for at in range(0, size, SLAB):
        length = min(SLAB, size - at)
        slab[:, at : at + length] = dot(hidden, down_w[:, at : at + length]).astype(BF16)
        columns = pl.ds(at, length)
        sends.append(fetch(slab.at[:, columns], out.at[:, columns], sent.at[cores + at // SLAB]))
    for copy in sends:
        copy.wait()


def expert(place, rows, mine, other, gate_proj, up_proj, down_proj, size, planes, cores, capacity):
    count, depth = rows.shape
    part, rest = mine.shape
    hidden = gate_proj.shape[2]
    width = down_proj.shape[2]
    block = count // (planes * cores)
    wide = (planes, cores, block, hidden)
    anywhere = pl.BlockSpec(memory_space=pl.ANY)
    return pl.pallas_call(
        expert_kernel,
        out_shape=(
            jax.ShapeDtypeStruct((count, size), BF16),
            jax.ShapeDtypeStruct((part, width - size), BF16),
            jax.ShapeDtypeStruct((part, width - size), BF16),
        ),
        in_specs=[pl.BlockSpec(memory_space=pltpu.SMEM)] + [anywhere] * 6,
        out_specs=[anywhere] * 3,
        scratch_shapes=[
            pltpu.VMEM((count, depth), BF16),
            pltpu.VMEM((2 * part, rest), BF16),
            pltpu.VMEM((depth + rest, hidden), BF16),
            pltpu.VMEM((depth + rest, hidden), BF16),
            pltpu.VMEM((hidden, width), BF16),
            pltpu.VMEM((2 * part, hidden), F32),
            pltpu.VMEM((2 * part, hidden), F32),
            pltpu.VMEM(wide, F32),
            pltpu.VMEM(wide, F32),
            pltpu.VMEM((cores, part, hidden), F32),
            pltpu.VMEM((count, size), BF16),
            pltpu.VMEM((cores, part, width - size), BF16),
            pltpu.SemaphoreType.DMA((4 * INNER + 5,)),
            pltpu.SemaphoreType.DMA((cores + pl.cdiv(size, SLAB),)),
        ],
        compiler_params=pltpu.CompilerParams(vmem_limit_bytes=60 << 20),
        cost_estimate=pl.CostEstimate(
            flops=6 * count * width * hidden,
            bytes_accessed=2 * count * (depth + size) + 6 * width * hidden,
            transcendentals=count * hidden,
        ),
    )(place, rows, mine, other, gate_proj, up_proj, down_proj)


def local(
    query_latent,
    query_rope,
    cache_latent,
    cache_rope,
    lengths,
    value_up,
    out_proj,
    residual,
    norm_gain,
    expert_ids,
    route_weights,
    gate_proj,
    up_proj,
    down_proj,
):
    row_count, width = residual.shape
    owners = lax.axis_size("ffn")
    cores = 2
    planes = lax.axis_size("attn") // cores
    core = lax.axis_index("attn") % cores
    plane = lax.axis_index("attn") // cores
    swap = [(a, a ^ 1) for a in range(planes * cores)]

    def from_plane(v, ahead):
        pairs = [
            (((y + ahead) % planes) * cores + c, y * cores + c)
            for y in range(planes)
            for c in range(cores)
        ]
        return lax.ppermute(v, "attn", pairs)

    def along_planes(v):
        return jnp.stack([v] + [from_plane(v, ahead) for ahead in range(1, planes)])

    named = expert_ids[:, :, None] == jnp.arange(owners, dtype=jnp.int32)[None, None, :]
    routed = jnp.sum(named.astype(F32), axis=1)
    weights = jnp.sum(jnp.where(named, route_weights[:, :, None], F32(0.0)), axis=1)
    capacity = min(row_count, row_count * expert_ids.shape[1] // owners + 1)

    def slots_of(routed, weight):
        rank = jnp.cumsum(routed, axis=-2) - routed
        routed, weight, rank = (jnp.moveaxis(v, -1, 0)[..., None, :] for v in (routed, weight, rank))
        slot = jnp.arange(capacity, dtype=jnp.int32).astype(F32)[:, None]
        placed = ((routed == 1.0) & (rank == slot)).astype(F32)
        return placed, placed * weight

    score_scale = (value_up.shape[2] + query_rope.shape[2]) ** (-0.5)
    pieces = attend(
        query_latent,
        query_rope,
        cache_latent,
        cache_rope,
        lengths,
        value_up,
        out_proj,
        score_scale,
        owners,
        PARTS,
    )
    eye = jnp.eye(planes, dtype=F32)

    def block_diagonal(v):
        spread = v[:, :, :, None, :] * eye[None, :, None, :, None]
        return spread.reshape(owners * planes * capacity, planes * row_count)

    placed, weighting = slots_of(routed, weights)
    placed = placed.reshape(owners * capacity, row_count).astype(BF16)
    weighting = weighting.reshape(owners * capacity, row_count)
    terms, left = [routed], weights
    for _ in range(3):
        term = lax.reduce_precision(left, 8, 7)
        terms.append(term)
        left = left - term
    table = jnp.pad(jnp.concatenate(terms, axis=1), ((0, 0), (0, 128 - 4 * owners))).astype(BF16)
    pieces = lax.all_to_all(pieces, "ffn", split_axis=0, concat_axis=0, tiled=True)
    attended = (
        jnp.sum(pieces.astype(F32), axis=0)
        .reshape(PARTS, row_count, width // PARTS)
        .transpose(1, 0, 2)
        .reshape(row_count, width)
    )
    mixed = residual.astype(F32) + attended
    inverse = lax.rsqrt(jnp.mean(mixed * mixed, axis=1, keepdims=True) + 1e-06)
    normed = (mixed * inverse * norm_gain.astype(F32)[None, :]).astype(BF16)

    outgoing = dot(placed, normed[:, :IN_RING]).astype(BF16).reshape(owners, capacity, IN_RING)
    near = jnp.concatenate([normed[:, IN_RING:], table], axis=1)
    arrived = lax.all_to_all(outgoing, "ffn", split_axis=0, concat_axis=0, tiled=True)
    arrived = arrived.reshape(owners * capacity, IN_RING)

    rest = width - IN_RING
    near, arrived = lax.optimization_barrier((near, arrived))
    near = along_planes(near)
    tables = near[:, :, rest:].astype(F32)
    tables = [tables[:, :, at * owners : (at + 1) * owners] for at in range(4)]
    placed_all, weighting_all = slots_of(tables[0], tables[1] + tables[2] + tables[3])
    placed_all = block_diagonal(placed_all).astype(BF16)
    weighting_all = block_diagonal(weighting_all)
    near = near[:, :, :rest].reshape(planes * row_count, rest)
    ring_rows = lax.all_gather(arrived, "attn", axis=0, tiled=True)
    outgoing = dot(placed_all, near).astype(BF16).reshape(owners, planes * capacity, rest)
    mine = lax.all_to_all(outgoing, "ffn", split_axis=0, concat_axis=0, tiled=True)
    mine = mine.reshape(owners * planes * capacity, rest)
    other = lax.ppermute(mine, "attn", swap)

    partial_value, theirs, ours = expert(
        jnp.stack([core, plane]),
        ring_rows,
        mine,
        other,
        gate_proj,
        up_proj,
        down_proj,
        OUT_RING,
        planes,
        cores,
        capacity,
    )
    summed = lax.psum_scatter(partial_value, "attn", scatter_dimension=0, tiled=True)

    rest = width - OUT_RING
    theirs = lax.ppermute(theirs, "attn", swap)
    ours = (ours.astype(F32) + theirs.astype(F32)).astype(BF16)
    ours = ours.reshape(owners, planes * capacity, rest)
    ours = lax.all_to_all(ours, "ffn", split_axis=0, concat_axis=0, tiled=True)
    ours = jnp.einsum(
        "sr,sd->rd",
        weighting_all,
        ours.reshape(owners * planes * capacity, rest).astype(F32),
        precision=lax.Precision.HIGHEST,
    ).astype(BF16)
    ours = ours.reshape(planes, row_count, rest)
    sum_rest = ours[0].astype(F32)
    for ahead in range(1, planes):
        sum_rest = sum_rest + from_plane(ours[planes - ahead], ahead).astype(F32)

    returned = lax.all_to_all(
        summed.reshape(owners, capacity, OUT_RING), "ffn", split_axis=0, concat_axis=0, tiled=True
    )
    sum_ring = jnp.einsum(
        "sr,sd->rd",
        weighting,
        returned.reshape(owners * capacity, OUT_RING).astype(F32),
        precision=lax.Precision.HIGHEST,
    )
    return (mixed + jnp.concatenate([sum_ring, sum_rest], axis=1)).astype(BF16)


def solution(mesh):
    return jax.shard_map(
        local,
        mesh=mesh,
        in_specs=(
            P("attn", "ffn", None),
            P("attn", "ffn", None),
            P("attn", None, None),
            P("attn", None, None),
            P("attn"),
            P("ffn", None, None),
            P("ffn", None, None),
            P(("attn", "ffn"), None),
            P(),
            P(("attn", "ffn"), None),
            P(("attn", "ffn"), None),
            P("ffn", None, "attn"),
            P("ffn", None, "attn"),
            P("ffn", "attn", None),
        ),
        out_specs=P(("attn", "ffn"), None),
        check_vma=False,
    )
```

```python
import math

import jax
import jax.numpy as jnp
from jax import lax
from jax.experimental import pallas as pl
from jax.experimental.pallas import tpu as pltpu
from jax.sharding import PartitionSpec as P

PARTS = 4
UNIT = 512
IN_RING = 3584
OUT_RING = 4096
F32 = jnp.float32
BF16 = jnp.bfloat16


def dot(a, b):
    return jnp.dot(a, b, preferred_element_type=F32)


GROUP = 4

def attend_kernel(
    scale,
    owners,
    parts,
    lengths,
    query,
    cache,
    query_rope,
    cache_rope,
    value_up,
    out_proj,
    out,
    rope,
    latent,
    values,
    weights,
    arrived,
):
    step = pl.program_id(0)
    heads = query.shape[1]
    depth, positions = cache.shape[2], cache.shape[1]
    rows = cache.shape[0]
    count = GROUP * heads
    width = weights.shape[1] // parts
    fetches = [
        pltpu.make_async_copy(
            out_proj.at[:, pl.ds(part * width, width)],
            weights.at[:, pl.ds(part * width, width)],
            arrived.at[part],
        )
        for part in range(parts)
    ]

    @pl.when(step == 0)
    def _():
        for fetch in fetches:
            fetch.start()
        for h in range(heads):
            vector = query_rope[h].astype(F32)
            parts = []
            for at in range(positions):
                parts.append(jnp.sum(vector * cache_rope[at].astype(F32), axis=0, keepdims=True))
            wide = jnp.concatenate(parts, axis=0).T
            rope[pl.ds(h, wide.shape[0], heads), :] = jnp.concatenate([wide] * 2, axis=1)

    groups = rows // GROUP
    total = rows * heads
    base = pl.multiple_of(step * total, total)
    keys = [
        cache[group * GROUP : (group + 1) * GROUP].reshape(GROUP * positions, depth)
        for group in range(groups)
    ]
    scores = []
    for group in range(groups):
        queries = jnp.concatenate([query[group * GROUP + i] for i in range(GROUP)], axis=0)
        scores.append(
            lax.dot_general(
                queries, keys[group], (((1,), (1,)), ((), ())), preferred_element_type=F32
            )
        )
    scores = jnp.concatenate(scores, axis=0)
    near = rope[pl.ds(base, total), :]
    scores = (scores + jnp.concatenate([near] * (GROUP // 2), axis=1)) * scale
    row = lax.broadcasted_iota(jnp.int32, scores.shape, 0) // heads
    own = lax.broadcasted_iota(jnp.int32, scores.shape, 1) - (row % GROUP) * positions
    limit = jnp.concatenate(
        [jnp.full((heads, GROUP * positions), lengths[step * rows + i], jnp.int32) for i in range(rows)],
        axis=0,
    )
    live = (own >= 0) & (own < limit)
    scores = jnp.where(live, scores, F32(-1e30))
    top = jnp.max(scores, axis=1, keepdims=True)
    expo = jnp.where(live, jnp.exp(scores - top), F32(0.0))
    probs = (expo / jnp.sum(expo, axis=1, keepdims=True)).astype(BF16)
    mixed = jnp.concatenate(
        [
            dot(probs[group * count : (group + 1) * count], keys[group])
            for group in range(groups)
        ],
        axis=0,
    )
    for part in range(depth // 128):
        latent[part, pl.ds(base, total), :] = mixed[:, part * 128 : (part + 1) * 128]

    @pl.when(step == pl.num_programs(0) - 1)
    def _():
        all_rows = values.shape[0]
        size = value_up.shape[2]
        for h in range(heads):
            mixed = jnp.concatenate(
                [latent[part, pl.ds(h, all_rows, heads), :] for part in range(depth // 128)], axis=1
            ).astype(BF16)
            values[:, h * size : (h + 1) * size] = dot(mixed, value_up[h]).astype(BF16)
        own_rows = all_rows // owners
        for part, fetch in enumerate(fetches):
            fetch.wait()
            result = dot(values[...], weights[:, part * width : (part + 1) * width]).astype(BF16)
            for f in range(owners):
                out[f, part * own_rows : (part + 1) * own_rows] = result[
                    f * own_rows : (f + 1) * own_rows
                ]


def attend(
    query, query_rope, cache, cache_rope, lengths, value_up, out_proj, scale, owners, parts, steps=2
):
    rows, heads, depth = query.shape
    positions = cache.shape[1]
    block = rows // steps
    size = heads * value_up.shape[2]
    width = out_proj.shape[2]
    shape = (owners, parts * (rows // owners), width // parts)
    whole = lambda shape: pl.BlockSpec(shape, lambda k, n: (0,) * len(shape))
    query_rope = jnp.transpose(query_rope, (1, 2, 0))
    cache_rope = jnp.transpose(cache_rope, (1, 2, 0))
    return pl.pallas_call(
        lambda *refs: attend_kernel(scale, owners, parts, *refs),
        out_shape=jax.ShapeDtypeStruct(shape, BF16),
        grid_spec=pltpu.PrefetchScalarGridSpec(
            num_scalar_prefetch=1,
            grid=(steps,),
            in_specs=[
                pl.BlockSpec((block, heads, depth), lambda k, n: (k, 0, 0)),
                pl.BlockSpec((block, positions, depth), lambda k, n: (k, 0, 0)),
                whole(query_rope.shape),
                whole(cache_rope.shape),
                whole(value_up.shape),
                pl.BlockSpec(memory_space=pl.ANY),
            ],
            out_specs=whole(shape),
            scratch_shapes=[
                pltpu.VMEM((rows * heads, 2 * positions), F32),
                pltpu.VMEM((depth // 128, rows * heads, 128), F32),
                pltpu.VMEM((rows, size), BF16),
                pltpu.VMEM((size, width), BF16),
                pltpu.SemaphoreType.DMA((parts,)),
            ],
        ),
        compiler_params=pltpu.CompilerParams(vmem_limit_bytes=60 << 20),
        cost_estimate=pl.CostEstimate(
            flops=4 * rows * heads * positions * depth * GROUP + 2 * rows * size * width,
            bytes_accessed=2 * rows * positions * depth + 2 * size * width,
            transcendentals=rows * heads * positions,
        ),
    )(lengths, query, cache, query_rope, cache_rope, value_up, out_proj.reshape(size, width))


OWNED = 4
INNER = 2


def expert_kernel(planes, cores, place, *refs):
    blocks = refs[: planes * cores]
    mine, other, gate_proj, up_proj, down_proj, *refs = refs[planes * cores :]
    outs, refs = refs[: planes * cores + cores], refs[planes * cores + cores :]
    x, x_rest, gate_w, up_w, down_w, *refs = refs
    gate_rest, up_rest, gate, up, spread, share_ring, share_rest = refs[:-3]
    row_sem, weight_sem, sent = refs[-3:]
    core, plane = place[0], place[1]
    depth, rest = x.shape[1], x_rest.shape[1]
    count = mine.shape[0]
    block = gate.shape[2]
    own = block // OWNED
    tile = depth // INNER
    size = share_ring.shape[2]

    def fetch(source, target, sem):
        copy = pltpu.make_async_copy(source, target, sem)
        copy.start()
        return copy

    def fetch_weights(at, start, length):
        rows_at = pl.ds(start, length)
        return [
            fetch(gate_proj.at[0, rows_at], gate_w.at[rows_at], weight_sem.at[2 * at]),
            fetch(up_proj.at[0, rows_at], up_w.at[rows_at], weight_sem.at[2 * at + 1]),
        ]

    def row_of(at):
        turn, c = at // cores, at % cores
        c = core if c == 0 else 1 - core
        return (plane + turn) % planes, c

    rest_waits = fetch_weights(INNER, depth, rest) + [
        fetch(mine, x_rest.at[pl.ds(0, count)], row_sem.at[INNER, 0]),
        fetch(other, x_rest.at[pl.ds(count, count)], row_sem.at[INNER, 1]),
    ]
    waits = []
    for at in range(INNER):
        columns = pl.ds(at * tile, tile)
        copies = fetch_weights(at, at * tile, tile)
        for i, ref in enumerate(blocks):
            y, c = row_of(i)
            target = x.at[pl.ds(pl.multiple_of((y * cores + c) * block, block), block), columns]
            copies.append(fetch(ref.at[:, columns], target, row_sem.at[at, i]))
        waits.append(copies)
    down_wait = fetch(down_proj.at[0], down_w, weight_sem.at[2 * INNER + 2])

    for copy in rest_waits:
        copy.wait()
    gate_rest[...] = dot(x_rest[...], gate_w[depth:])
    up_rest[...] = dot(x_rest[...], up_w[depth:])
    shape = gate.shape
    for at in range(INNER):
        for copy in waits[at]:
            copy.wait()
        start = at * tile
        part = x[:, start : start + tile]
        gate_part = dot(part, gate_w[start : start + tile]).reshape(shape)
        up_part = dot(part, up_w[start : start + tile]).reshape(shape)
        if at == 0:
            gate[...] = gate_part
            up[...] = up_part
        else:
            gate[...] += gate_part
            up[...] += up_part
    for i in range(planes * cores):
        y, c = row_of(i)
        turn, at = i // cores, i % cores
        for f in range(own):
            start = at * count + (f * planes + turn) * OWNED
            target = slice(f * OWNED, (f + 1) * OWNED)
            gate[y, c, target] += gate_rest[start : start + OWNED]
            up[y, c, target] += up_rest[start : start + OWNED]
    gated = gate[...]
    gate[...] = gated * jax.nn.sigmoid(gated) * up[...]
    down_wait.wait()
    sends = []
    for at in range(cores - 1, -1, -1):
        pieces = []
        for turn in range(planes):
            y, c = row_of(turn * cores + at)
            pieces.append(gate[y, c])
            for f in range(own):
                start = (f * planes + turn) * OWNED
                spread[at, start : start + OWNED] = gate[y, c, f * OWNED : (f + 1) * OWNED]
        ring = jnp.concatenate(pieces, axis=0).astype(BF16)
        share_ring[at] = dot(ring, down_w[:, :size]).astype(BF16)
        for turn in range(planes):
            i = at * planes + turn
            piece = share_ring.at[at, pl.ds(turn * block, block)]
            sends.append(fetch(piece, outs[i], sent.at[i]))
    for at in range(cores - 1, -1, -1):
        share_rest[at] = dot(spread[at].astype(BF16), down_w[:, size:]).astype(BF16)
        sends.append(fetch(share_rest.at[at], outs[planes * cores + at], sent.at[planes * cores + at]))
    for copy in sends:
        copy.wait()


def expert(place, blocks, mine, other, gate_proj, up_proj, down_proj, size, planes, cores):
    block, depth = blocks[0].shape
    count = planes * cores * block
    part, rest = mine.shape
    hidden = gate_proj.shape[2]
    width = down_proj.shape[2]
    wide = (planes, cores, block, hidden)
    anywhere = pl.BlockSpec(memory_space=pl.ANY)
    return pl.pallas_call(
        lambda *refs: expert_kernel(planes, cores, *refs),
        out_shape=[jax.ShapeDtypeStruct((block, size), BF16)] * (planes * cores)
        + [jax.ShapeDtypeStruct((part, width - size), BF16)] * cores,
        in_specs=[pl.BlockSpec(memory_space=pltpu.SMEM)] + [anywhere] * (len(blocks) + 5),
        out_specs=[anywhere] * (planes * cores + cores),
        scratch_shapes=[
            pltpu.VMEM((count, depth), BF16),
            pltpu.VMEM((2 * part, rest), BF16),
            pltpu.VMEM((depth + rest, hidden), BF16),
            pltpu.VMEM((depth + rest, hidden), BF16),
            pltpu.VMEM((hidden, width), BF16),
            pltpu.VMEM((2 * part, hidden), F32),
            pltpu.VMEM((2 * part, hidden), F32),
            pltpu.VMEM(wide, F32),
            pltpu.VMEM(wide, F32),
            pltpu.VMEM((cores, part, hidden), F32),
            pltpu.VMEM((cores, part, size), BF16),
            pltpu.VMEM((cores, part, width - size), BF16),
            pltpu.SemaphoreType.DMA((INNER + 1, len(blocks))),
            pltpu.SemaphoreType.DMA((2 * INNER + 3,)),
            pltpu.SemaphoreType.DMA((planes * cores + cores,)),
        ],
        compiler_params=pltpu.CompilerParams(vmem_limit_bytes=60 << 20),
        cost_estimate=pl.CostEstimate(
            flops=6 * count * width * hidden,
            bytes_accessed=4 * count * width + 6 * width * hidden,
            transcendentals=count * hidden,
        ),
    )(place, *blocks, mine, other, gate_proj, up_proj, down_proj)


def local(
    query_latent,
    query_rope,
    cache_latent,
    cache_rope,
    lengths,
    value_up,
    out_proj,
    residual,
    norm_gain,
    expert_ids,
    route_weights,
    gate_proj,
    up_proj,
    down_proj,
):
    row_count, width = residual.shape
    owners = lax.axis_size("ffn")
    cores = 2
    planes = lax.axis_size("attn") // cores
    core = lax.axis_index("attn") % cores
    plane = lax.axis_index("attn") // cores
    swap = [(a, a ^ 1) for a in range(planes * cores)]

    def from_plane(v, ahead):
        pairs = [
            (((y + ahead) % planes) * cores + c, y * cores + c)
            for y in range(planes)
            for c in range(cores)
        ]
        return lax.ppermute(v, "attn", pairs)

    def along_planes(v):
        return jnp.stack([v] + [from_plane(v, ahead) for ahead in range(1, planes)])

    named = expert_ids[:, :, None] == jnp.arange(owners, dtype=jnp.int32)[None, None, :]
    routed = jnp.sum(named.astype(F32), axis=1)
    weights = jnp.sum(jnp.where(named, route_weights[:, :, None], F32(0.0)), axis=1)
    capacity = min(row_count, row_count * expert_ids.shape[1] // owners + 1)

    def slots_of(routed, weight):
        rank = jnp.cumsum(routed, axis=-2) - routed
        routed, weight, rank = (jnp.moveaxis(v, -1, 0)[..., None, :] for v in (routed, weight, rank))
        slot = jnp.arange(capacity, dtype=jnp.int32).astype(F32)[:, None]
        placed = ((routed == 1.0) & (rank == slot)).astype(F32)
        return placed, placed * weight

    score_scale = (value_up.shape[2] + query_rope.shape[2]) ** (-0.5)
    pieces = attend(
        query_latent,
        query_rope,
        cache_latent,
        cache_rope,
        lengths,
        value_up,
        out_proj,
        score_scale,
        owners,
        PARTS,
    )
    eye = jnp.eye(planes, dtype=F32)

    def block_diagonal(v):
        spread = v[:, :, :, None, :] * eye[None, :, None, :, None]
        return spread.reshape(owners * planes * capacity, planes * row_count)

    placed, weighting = slots_of(routed, weights)
    placed = placed.reshape(owners * capacity, row_count).astype(BF16)
    weighting = weighting.reshape(owners * capacity, row_count)
    terms, left = [routed], weights
    for _ in range(3):
        term = lax.reduce_precision(left, 8, 7)
        terms.append(term)
        left = left - term
    table = jnp.pad(jnp.concatenate(terms, axis=1), ((0, 0), (0, 128 - 4 * owners))).astype(BF16)
    pieces = lax.all_to_all(pieces, "ffn", split_axis=0, concat_axis=0, tiled=True)
    attended = (
        jnp.sum(pieces.astype(F32), axis=0)
        .reshape(PARTS, row_count, width // PARTS)
        .transpose(1, 0, 2)
        .reshape(row_count, width)
    )
    mixed = residual.astype(F32) + attended
    inverse = lax.rsqrt(jnp.mean(mixed * mixed, axis=1, keepdims=True) + 1e-06)
    normed = (mixed * inverse * norm_gain.astype(F32)[None, :]).astype(BF16)

    outgoing = dot(placed, normed[:, :IN_RING]).astype(BF16).reshape(owners, capacity, IN_RING)
    near = jnp.concatenate([normed[:, IN_RING:], table], axis=1)
    arrived = lax.all_to_all(outgoing, "ffn", split_axis=0, concat_axis=0, tiled=True)
    arrived = arrived.reshape(owners * capacity, IN_RING)

    rest = width - IN_RING
    by_plane = [arrived] + [from_plane(arrived, ahead) for ahead in range(1, planes)]
    near = along_planes(near)
    tables = near[:, :, rest:].astype(F32)
    tables = [tables[:, :, at * owners : (at + 1) * owners] for at in range(4)]
    placed_all, weighting_all = slots_of(tables[0], tables[1] + tables[2] + tables[3])
    placed_all = block_diagonal(placed_all).astype(BF16)
    weighting_all = block_diagonal(weighting_all)
    near = near[:, :, :rest].reshape(planes * row_count, rest)
    outgoing = dot(placed_all, near).astype(BF16).reshape(owners, planes * capacity, rest)
    mine = lax.all_to_all(outgoing, "ffn", split_axis=0, concat_axis=0, tiled=True)
    *_, mine = lax.optimization_barrier((*by_plane, mine))
    blocks = [v for held in by_plane for v in (held, lax.ppermute(held, "attn", swap))]
    mine = mine.reshape(owners * planes * capacity, rest)
    other = lax.ppermute(mine, "attn", swap)

    *pieces, ours, theirs = expert(
        jnp.stack([core, plane]),
        blocks,
        mine,
        other,
        gate_proj,
        up_proj,
        down_proj,
        OUT_RING,
        planes,
        cores,
    )

    def add(a, b):
        return (a.astype(F32) + b.astype(F32)).astype(BF16)

    ring = {}
    for turn in (2, 1, 3, 0):
        ring[turn] = add(pieces[turn], lax.ppermute(pieces[planes + turn], "attn", swap))
    summed = ring[0].astype(F32)
    for ahead in range(1, planes):
        summed = summed + from_plane(ring[planes - ahead], ahead).astype(F32)
    summed = summed.astype(BF16)

    rest = width - OUT_RING
    ours = add(ours, lax.ppermute(theirs, "attn", swap))
    ours = ours.reshape(owners, planes * capacity, rest)
    ours = lax.all_to_all(ours, "ffn", split_axis=0, concat_axis=0, tiled=True)
    ours = jnp.einsum(
        "sr,sd->rd",
        weighting_all,
        ours.reshape(owners * planes * capacity, rest).astype(F32),
        precision=lax.Precision.HIGHEST,
    ).astype(BF16)
    ours = ours.reshape(planes, row_count, rest)
    sum_rest = ours[0].astype(F32)
    for ahead in range(1, planes):
        sum_rest = sum_rest + from_plane(ours[planes - ahead], ahead).astype(F32)

    returned = lax.all_to_all(
        summed.reshape(owners, capacity, OUT_RING), "ffn", split_axis=0, concat_axis=0, tiled=True
    )
    sum_ring = jnp.einsum(
        "sr,sd->rd",
        weighting,
        returned.reshape(owners * capacity, OUT_RING).astype(F32),
        precision=lax.Precision.HIGHEST,
    )
    return (mixed + jnp.concatenate([sum_ring, sum_rest], axis=1)).astype(BF16)


def solution(mesh):
    return jax.shard_map(
        local,
        mesh=mesh,
        in_specs=(
            P("attn", "ffn", None),
            P("attn", "ffn", None),
            P("attn", None, None),
            P("attn", None, None),
            P("attn"),
            P("ffn", None, None),
            P("ffn", None, None),
            P(("attn", "ffn"), None),
            P(),
            P(("attn", "ffn"), None),
            P(("attn", "ffn"), None),
            P("ffn", None, "attn"),
            P("ffn", None, "attn"),
            P("ffn", "attn", None),
        ),
        out_specs=P(("attn", "ffn"), None),
        check_vma=False,
    )
```

```python
import math

import jax
import jax.numpy as jnp
from jax import lax
from jax.experimental import pallas as pl
from jax.experimental.pallas import tpu as pltpu
from jax.sharding import PartitionSpec as P

PARTS = 4
UNIT = 512
IN_RING = 3584
OUT_RING = 4096
F32 = jnp.float32
BF16 = jnp.bfloat16


def dot(a, b):
    return jnp.dot(a, b, preferred_element_type=F32)


GROUP = 4

def attend_kernel(
    scale,
    owners,
    parts,
    lengths,
    query,
    cache,
    query_rope,
    cache_rope,
    value_up,
    out_proj,
    out,
    rope,
    latent,
    values,
    weights,
    arrived,
):
    step = pl.program_id(0)
    heads = query.shape[1]
    depth, positions = cache.shape[2], cache.shape[1]
    rows = cache.shape[0]
    count = GROUP * heads
    width = weights.shape[1] // parts
    fetches = [
        pltpu.make_async_copy(
            out_proj.at[:, pl.ds(part * width, width)],
            weights.at[:, pl.ds(part * width, width)],
            arrived.at[part],
        )
        for part in range(parts)
    ]

    @pl.when(step == 0)
    def _():
        for fetch in fetches:
            fetch.start()
        for h in range(heads):
            vector = query_rope[h].astype(F32)
            parts = []
            for at in range(positions):
                parts.append(jnp.sum(vector * cache_rope[at].astype(F32), axis=0, keepdims=True))
            wide = jnp.concatenate(parts, axis=0).T
            rope[pl.ds(h, wide.shape[0], heads), :] = jnp.concatenate([wide] * 2, axis=1)

    groups = rows // GROUP
    total = rows * heads
    base = pl.multiple_of(step * total, total)
    keys = [
        cache[group * GROUP : (group + 1) * GROUP].reshape(GROUP * positions, depth)
        for group in range(groups)
    ]
    scores = []
    for group in range(groups):
        queries = jnp.concatenate([query[group * GROUP + i] for i in range(GROUP)], axis=0)
        scores.append(
            lax.dot_general(
                queries, keys[group], (((1,), (1,)), ((), ())), preferred_element_type=F32
            )
        )
    scores = jnp.concatenate(scores, axis=0)
    near = rope[pl.ds(base, total), :]
    scores = (scores + jnp.concatenate([near] * (GROUP // 2), axis=1)) * scale
    row = lax.broadcasted_iota(jnp.int32, scores.shape, 0) // heads
    own = lax.broadcasted_iota(jnp.int32, scores.shape, 1) - (row % GROUP) * positions
    limit = jnp.concatenate(
        [jnp.full((heads, GROUP * positions), lengths[step * rows + i], jnp.int32) for i in range(rows)],
        axis=0,
    )
    live = (own >= 0) & (own < limit)
    scores = jnp.where(live, scores, F32(-1e30))
    top = jnp.max(scores, axis=1, keepdims=True)
    expo = jnp.where(live, jnp.exp(scores - top), F32(0.0))
    probs = (expo / jnp.sum(expo, axis=1, keepdims=True)).astype(BF16)
    mixed = jnp.concatenate(
        [
            dot(probs[group * count : (group + 1) * count], keys[group])
            for group in range(groups)
        ],
        axis=0,
    )
    for part in range(depth // 128):
        latent[part, pl.ds(base, total), :] = mixed[:, part * 128 : (part + 1) * 128]

    @pl.when(step == pl.num_programs(0) - 1)
    def _():
        all_rows = values.shape[0]
        size = value_up.shape[2]
        for h in range(heads):
            mixed = jnp.concatenate(
                [latent[part, pl.ds(h, all_rows, heads), :] for part in range(depth // 128)], axis=1
            ).astype(BF16)
            values[:, h * size : (h + 1) * size] = dot(mixed, value_up[h]).astype(BF16)
        own_rows = all_rows // owners
        for part, fetch in enumerate(fetches):
            fetch.wait()
            result = dot(values[...], weights[:, part * width : (part + 1) * width]).astype(BF16)
            for f in range(owners):
                out[f, part * own_rows : (part + 1) * own_rows] = result[
                    f * own_rows : (f + 1) * own_rows
                ]


def attend(
    query, query_rope, cache, cache_rope, lengths, value_up, out_proj, scale, owners, parts, steps=2
):
    rows, heads, depth = query.shape
    positions = cache.shape[1]
    block = rows // steps
    size = heads * value_up.shape[2]
    width = out_proj.shape[2]
    shape = (owners, parts * (rows // owners), width // parts)
    whole = lambda shape: pl.BlockSpec(shape, lambda k, n: (0,) * len(shape))
    query_rope = jnp.transpose(query_rope, (1, 2, 0))
    cache_rope = jnp.transpose(cache_rope, (1, 2, 0))
    return pl.pallas_call(
        lambda *refs: attend_kernel(scale, owners, parts, *refs),
        out_shape=jax.ShapeDtypeStruct(shape, BF16),
        grid_spec=pltpu.PrefetchScalarGridSpec(
            num_scalar_prefetch=1,
            grid=(steps,),
            in_specs=[
                pl.BlockSpec((block, heads, depth), lambda k, n: (k, 0, 0)),
                pl.BlockSpec((block, positions, depth), lambda k, n: (k, 0, 0)),
                whole(query_rope.shape),
                whole(cache_rope.shape),
                whole(value_up.shape),
                pl.BlockSpec(memory_space=pl.ANY),
            ],
            out_specs=whole(shape),
            scratch_shapes=[
                pltpu.VMEM((rows * heads, 2 * positions), F32),
                pltpu.VMEM((depth // 128, rows * heads, 128), F32),
                pltpu.VMEM((rows, size), BF16),
                pltpu.VMEM((size, width), BF16),
                pltpu.SemaphoreType.DMA((parts,)),
            ],
        ),
        compiler_params=pltpu.CompilerParams(vmem_limit_bytes=60 << 20),
        cost_estimate=pl.CostEstimate(
            flops=4 * rows * heads * positions * depth * GROUP + 2 * rows * size * width,
            bytes_accessed=2 * rows * positions * depth + 2 * size * width,
            transcendentals=rows * heads * positions,
        ),
    )(lengths, query, cache, query_rope, cache_rope, value_up, out_proj.reshape(size, width))


OWNED = 4
SLAB = 2048
INNER = 2


def expert_kernel(planes, sides, *refs):
    blocks, refs = refs[:planes], refs[planes:]
    mine, refs = refs[0], refs[1:]
    weights = [refs[3 * side : 3 * side + 3] for side in range(sides)]
    refs = refs[3 * sides :]
    outs, refs = refs[: planes + 1], refs[planes + 1 :]
    x, x_rest, gate_w, up_w, down_w, *refs = refs
    gate_rest, up_rest, gate, up, spread, share_ring, share_rest = refs[:-3]
    row_sem, weight_sem, sent = refs[-3:]
    depth, rest = x.shape[1], x_rest.shape[1]
    block = gate.shape[1]
    own = block // OWNED
    tile = depth // INNER
    size = share_ring.shape[1]
    half = gate_w.shape[1] // sides

    def fetch(source, target, sem):
        copy = pltpu.make_async_copy(source, target, sem)
        copy.start()
        return copy

    def fetch_weights(at, start, length):
        rows_at = pl.ds(start, length)
        copies = []
        for side in range(sides):
            columns = pl.ds(side * half, half)
            for i, target in enumerate((gate_w, up_w)):
                source = weights[side][i].at[0, rows_at]
                copies.append(
                    fetch(source, target.at[rows_at, columns], weight_sem.at[at, 2 * side + i])
                )
        return copies

    rest_waits = fetch_weights(INNER, depth, rest) + [fetch(mine, x_rest, row_sem.at[INNER, 0])]
    waits = []
    for at in range(INNER):
        columns = pl.ds(at * tile, tile)
        copies = fetch_weights(at, at * tile, tile)
        for i, ref in enumerate(blocks):
            target = x.at[pl.ds(i * block, block), columns]
            copies.append(fetch(ref.at[:, columns], target, row_sem.at[at, i]))
        waits.append(copies)
    down_waits = [
        fetch(weights[side][2].at[0], down_w.at[pl.ds(side * half, half)], weight_sem.at[INNER + 1, side])
        for side in range(sides)
    ]

    for copy in rest_waits:
        copy.wait()
    gate_rest[...] = dot(x_rest[...], gate_w[depth:])
    up_rest[...] = dot(x_rest[...], up_w[depth:])
    shape = gate.shape
    for at in range(INNER):
        for copy in waits[at]:
            copy.wait()
        start = at * tile
        part = x[:, start : start + tile]
        gate_part = dot(part, gate_w[start : start + tile]).reshape(shape)
        up_part = dot(part, up_w[start : start + tile]).reshape(shape)
        if at == 0:
            gate[...] = gate_part
            up[...] = up_part
        else:
            gate[...] += gate_part
            up[...] += up_part
    for turn in range(planes):
        for f in range(own):
            start = (f * planes + turn) * OWNED
            target = slice(f * OWNED, (f + 1) * OWNED)
            gate[turn, target] += gate_rest[start : start + OWNED]
            up[turn, target] += up_rest[start : start + OWNED]
    gated = gate[...]
    hidden = gated * jax.nn.sigmoid(gated) * up[...]
    gate[...] = hidden
    for copy in down_waits:
        copy.wait()
    hidden = hidden.reshape(planes * block, gate.shape[2]).astype(BF16)
    sends = []
    for at in range(0, size, SLAB):
        columns = slice(at, min(at + SLAB, size))
        share_ring[:, columns] = dot(hidden, down_w[:, columns]).astype(BF16)
    for turn in range(planes):
        piece = share_ring.at[pl.ds(turn * block, block)]
        sends.append(fetch(piece, outs[turn], sent.at[turn]))
        for f in range(own):
            start = (f * planes + turn) * OWNED
            spread[start : start + OWNED] = gate[turn, f * OWNED : (f + 1) * OWNED]
    share_rest[...] = dot(spread[...].astype(BF16), down_w[:, size:]).astype(BF16)
    sends.append(fetch(share_rest, outs[planes], sent.at[planes]))
    for copy in sends:
        copy.wait()


def expert(blocks, mine, weights, size):
    planes, sides = len(blocks), len(weights)
    block, depth = blocks[0].shape
    count, rest = mine.shape
    hidden = sides * weights[0][0].shape[2]
    width = weights[0][2].shape[2]
    wide = (planes, block, hidden)
    anywhere = pl.BlockSpec(memory_space=pl.ANY)
    return pl.pallas_call(
        lambda *refs: expert_kernel(planes, sides, *refs),
        out_shape=[jax.ShapeDtypeStruct((block, size), BF16)] * planes
        + [jax.ShapeDtypeStruct((count, width - size), BF16)],
        in_specs=[anywhere] * (planes + 1 + 3 * sides),
        out_specs=[anywhere] * (planes + 1),
        scratch_shapes=[
            pltpu.VMEM((count, depth), BF16),
            pltpu.VMEM((count, rest), BF16),
            pltpu.VMEM((depth + rest, hidden), BF16),
            pltpu.VMEM((depth + rest, hidden), BF16),
            pltpu.VMEM((hidden, width), BF16),
            pltpu.VMEM((count, hidden), F32),
            pltpu.VMEM((count, hidden), F32),
            pltpu.VMEM(wide, F32),
            pltpu.VMEM(wide, F32),
            pltpu.VMEM((count, hidden), F32),
            pltpu.VMEM((count, size), BF16),
            pltpu.VMEM((count, width - size), BF16),
            pltpu.SemaphoreType.DMA((INNER + 1, planes)),
            pltpu.SemaphoreType.DMA((INNER + 2, 2 * sides)),
            pltpu.SemaphoreType.DMA((planes + 1,)),
        ],
        compiler_params=pltpu.CompilerParams(vmem_limit_bytes=60 << 20),
        cost_estimate=pl.CostEstimate(
            flops=6 * count * width * hidden,
            bytes_accessed=4 * count * width + 6 * width * hidden,
            transcendentals=count * hidden,
        ),
    )(*blocks, mine, *[v for side in weights for v in side])


def local(
    query_latent,
    query_rope,
    cache_latent,
    cache_rope,
    lengths,
    value_up,
    out_proj,
    residual,
    norm_gain,
    expert_ids,
    route_weights,
    gate_proj,
    up_proj,
    down_proj,
):
    row_count, width = residual.shape
    owners = lax.axis_size("ffn")
    cores = 2
    planes = lax.axis_size("attn") // cores
    swap = [(a, a ^ 1) for a in range(planes * cores)]

    def from_plane(v, ahead):
        pairs = [
            (((y + ahead) % planes) * cores + c, y * cores + c)
            for y in range(planes)
            for c in range(cores)
        ]
        return lax.ppermute(v, "attn", pairs)

    def along_planes(v):
        return jnp.stack([v] + [from_plane(v, ahead) for ahead in range(1, planes)])

    named = expert_ids[:, :, None] == jnp.arange(owners, dtype=jnp.int32)[None, None, :]
    routed = jnp.sum(named.astype(F32), axis=1)
    weights = jnp.sum(jnp.where(named, route_weights[:, :, None], F32(0.0)), axis=1)
    capacity = min(row_count, row_count * expert_ids.shape[1] // owners + 1)

    def slots_of(routed, weight):
        rank = jnp.cumsum(routed, axis=-2) - routed
        routed, weight, rank = (jnp.moveaxis(v, -1, 0)[..., None, :] for v in (routed, weight, rank))
        slot = jnp.arange(capacity, dtype=jnp.int32).astype(F32)[:, None]
        placed = ((routed == 1.0) & (rank == slot)).astype(F32)
        return placed, placed * weight

    score_scale = (value_up.shape[2] + query_rope.shape[2]) ** (-0.5)
    pieces = attend(
        query_latent,
        query_rope,
        cache_latent,
        cache_rope,
        lengths,
        value_up,
        out_proj,
        score_scale,
        owners,
        PARTS,
    )
    eye = jnp.eye(planes, dtype=F32)

    def block_diagonal(v):
        spread = v[:, :, :, None, :] * eye[None, :, None, :, None]
        return spread.reshape(owners * planes * capacity, planes * row_count)

    placed, weighting = slots_of(routed, weights)
    placed = placed.reshape(owners * capacity, row_count).astype(BF16)
    weighting = weighting.reshape(owners * capacity, row_count)
    terms, left = [routed], weights
    for _ in range(3):
        term = lax.reduce_precision(left, 8, 7)
        terms.append(term)
        left = left - term
    table = jnp.pad(jnp.concatenate(terms, axis=1), ((0, 0), (0, 128 - 4 * owners))).astype(BF16)
    pieces = lax.all_to_all(pieces, "ffn", split_axis=0, concat_axis=0, tiled=True)
    weights_here = (gate_proj, up_proj, down_proj)
    weights_there = [lax.ppermute(v, "attn", swap) for v in weights_here]
    pieces, weights_there = lax.optimization_barrier((pieces, weights_there))
    attended = (
        jnp.sum(pieces.astype(F32), axis=0)
        .reshape(PARTS, row_count, width // PARTS)
        .transpose(1, 0, 2)
        .reshape(row_count, width)
    )
    mixed = residual.astype(F32) + attended
    inverse = lax.rsqrt(jnp.mean(mixed * mixed, axis=1, keepdims=True) + 1e-06)
    normed = (mixed * inverse * norm_gain.astype(F32)[None, :]).astype(BF16)

    outgoing = dot(placed, normed[:, :IN_RING]).astype(BF16).reshape(owners, capacity, IN_RING)
    near = jnp.concatenate([normed[:, IN_RING:], table], axis=1)
    arrived = lax.all_to_all(outgoing, "ffn", split_axis=0, concat_axis=0, tiled=True)
    arrived = arrived.reshape(owners * capacity, IN_RING)

    rest = width - IN_RING
    by_plane = [arrived] + [from_plane(arrived, ahead) for ahead in range(1, planes)]
    near = along_planes(near)
    tables = near[:, :, rest:].astype(F32)
    tables = [tables[:, :, at * owners : (at + 1) * owners] for at in range(4)]
    placed_all, weighting_all = slots_of(tables[0], tables[1] + tables[2] + tables[3])
    placed_all = block_diagonal(placed_all).astype(BF16)
    weighting_all = block_diagonal(weighting_all)
    near = near[:, :, :rest].reshape(planes * row_count, rest)
    outgoing = dot(placed_all, near).astype(BF16).reshape(owners, planes * capacity, rest)
    mine = lax.all_to_all(outgoing, "ffn", split_axis=0, concat_axis=0, tiled=True)
    *by_plane, mine = lax.optimization_barrier((*by_plane, mine))
    mine = mine.reshape(owners * planes * capacity, rest)
    *ring, ours = expert(by_plane, mine, (weights_here, weights_there), OUT_RING)

    summed = ring[0].astype(F32)
    for ahead in range(1, planes):
        summed = summed + from_plane(ring[planes - ahead], ahead).astype(F32)
    summed = summed.astype(BF16)

    rest = width - OUT_RING
    ours = ours.reshape(owners, planes * capacity, rest)
    ours = lax.all_to_all(ours, "ffn", split_axis=0, concat_axis=0, tiled=True)
    ours = jnp.einsum(
        "sr,sd->rd",
        weighting_all,
        ours.reshape(owners * planes * capacity, rest).astype(F32),
        precision=lax.Precision.HIGHEST,
    ).astype(BF16)
    ours = ours.reshape(planes, row_count, rest)
    sum_rest = ours[0].astype(F32)
    for ahead in range(1, planes):
        sum_rest = sum_rest + from_plane(ours[planes - ahead], ahead).astype(F32)

    returned = lax.all_to_all(
        summed.reshape(owners, capacity, OUT_RING), "ffn", split_axis=0, concat_axis=0, tiled=True
    )
    sum_ring = jnp.einsum(
        "sr,sd->rd",
        weighting,
        returned.reshape(owners * capacity, OUT_RING).astype(F32),
        precision=lax.Precision.HIGHEST,
    )
    return (mixed + jnp.concatenate([sum_ring, sum_rest], axis=1)).astype(BF16)


def solution(mesh):
    return jax.shard_map(
        local,
        mesh=mesh,
        in_specs=(
            P("attn", "ffn", None),
            P("attn", "ffn", None),
            P("attn", None, None),
            P("attn", None, None),
            P("attn"),
            P("ffn", None, None),
            P("ffn", None, None),
            P(("attn", "ffn"), None),
            P(),
            P(("attn", "ffn"), None),
            P(("attn", "ffn"), None),
            P("ffn", None, "attn"),
            P("ffn", None, "attn"),
            P("ffn", "attn", None),
        ),
        out_specs=P(("attn", "ffn"), None),
        check_vma=False,
    )
```

```python
import math

import jax
import jax.numpy as jnp
from jax import lax
from jax.experimental import pallas as pl
from jax.experimental.pallas import tpu as pltpu
from jax.sharding import PartitionSpec as P

PARTS = 4
UNIT = 512
IN_RING = 3072
OUT_RING = 4096
F32 = jnp.float32
BF16 = jnp.bfloat16


def dot(a, b):
    return jnp.dot(a, b, preferred_element_type=F32)


GROUP = 4
STEPS = 3

def attend_kernel(
    scale,
    owners,
    parts,
    lengths,
    query,
    cache_here,
    query_rope,
    cache_rope,
    value_here,
    out_proj,
    out,
    rope,
    latent,
    values,
    weights,
    cache,
    value_up,
    arrived,
):
    all_rows, heads, depth = query.shape
    positions = cache.shape[1]
    rows = all_rows // STEPS
    count = GROUP * heads
    width = weights.shape[1] // parts

    def fetch(source, target, at):
        copy = pltpu.make_async_copy(source, target, arrived.at[at])
        copy.start()
        return copy

    chunks = []
    for step in range(STEPS):
        here = pl.ds(step * rows, rows)
        chunks.append(fetch(cache_here.at[here], cache.at[here], step))
    value_fetch = fetch(value_here, value_up, STEPS)
    fetches = []
    for part in range(parts):
        columns = pl.ds(part * width, width)
        fetches.append(
            fetch(out_proj.at[:, columns], weights.at[:, columns], STEPS + 1 + part)
        )

    for h in range(heads):
        vector = query_rope[h].astype(F32)
        terms = []
        for at in range(positions):
            terms.append(jnp.sum(vector * cache_rope[at].astype(F32), axis=0, keepdims=True))
        wide = jnp.concatenate(terms, axis=0).T
        rope[pl.ds(h, all_rows, heads), :] = jnp.concatenate([wide] * 2, axis=1)

    groups = rows // GROUP
    total = rows * heads
    for step in range(STEPS):
        chunks[step].wait()
        first = step * rows
        base = step * total
        keys = [
            cache[first + group * GROUP : first + (group + 1) * GROUP].reshape(
                GROUP * positions, depth
            )
            for group in range(groups)
        ]
        scores = []
        for group in range(groups):
            queries = jnp.concatenate(
                [query[first + group * GROUP + i] for i in range(GROUP)], axis=0
            )
            scores.append(
                lax.dot_general(
                    queries, keys[group], (((1,), (1,)), ((), ())), preferred_element_type=F32
                )
            )
        scores = jnp.concatenate(scores, axis=0)
        near = rope[base : base + total, :]
        scores = (scores + jnp.concatenate([near] * (GROUP // 2), axis=1)) * scale
        row = lax.broadcasted_iota(jnp.int32, scores.shape, 0) // heads
        own = lax.broadcasted_iota(jnp.int32, scores.shape, 1) - (row % GROUP) * positions
        limit = jnp.concatenate(
            [
                jnp.full((heads, GROUP * positions), lengths[first + i], jnp.int32)
                for i in range(rows)
            ],
            axis=0,
        )
        live = (own >= 0) & (own < limit)
        scores = jnp.where(live, scores, F32(-1e30))
        top = jnp.max(scores, axis=1, keepdims=True)
        expo = jnp.where(live, jnp.exp(scores - top), F32(0.0))
        probs = (expo / jnp.sum(expo, axis=1, keepdims=True)).astype(BF16)
        mixed = jnp.concatenate(
            [
                dot(probs[group * count : (group + 1) * count], keys[group])
                for group in range(groups)
            ],
            axis=0,
        )
        for part in range(depth // 128):
            latent[part, base : base + total, :] = mixed[:, part * 128 : (part + 1) * 128]

    value_fetch.wait()
    size = value_up.shape[2]
    for h in range(heads):
        mixed = jnp.concatenate(
            [latent[part, pl.ds(h, all_rows, heads), :] for part in range(depth // 128)], axis=1
        ).astype(BF16)
        values[:, h * size : (h + 1) * size] = dot(mixed, value_up[h]).astype(BF16)
    own_rows = all_rows // owners
    for part, copy in enumerate(fetches):
        copy.wait()
        result = dot(values[...], weights[:, part * width : (part + 1) * width]).astype(BF16)
        for f in range(owners):
            out[f, part * own_rows : (part + 1) * own_rows] = result[
                f * own_rows : (f + 1) * own_rows
            ]


def attend(query, query_rope, cache, cache_rope, lengths, value_up, out_proj, scale, owners, parts):
    rows, heads, depth = query.shape
    positions = cache.shape[1]
    size = heads * value_up.shape[2]
    width = out_proj.shape[2]
    shape = (owners, parts * (rows // owners), width // parts)
    anywhere = pl.BlockSpec(memory_space=pl.ANY)
    inside = pl.BlockSpec(memory_space=pltpu.VMEM)
    query_rope = jnp.transpose(query_rope, (1, 2, 0))
    cache_rope = jnp.transpose(cache_rope, (1, 2, 0))
    return pl.pallas_call(
        lambda *refs: attend_kernel(scale, owners, parts, *refs),
        out_shape=jax.ShapeDtypeStruct(shape, BF16),
        in_specs=[
            pl.BlockSpec(memory_space=pltpu.SMEM),
            inside,
            anywhere,
            inside,
            inside,
            anywhere,
            anywhere,
        ],
        out_specs=inside,
        scratch_shapes=[
            pltpu.VMEM((rows * heads, 2 * positions), F32),
            pltpu.VMEM((depth // 128, rows * heads, 128), F32),
            pltpu.VMEM((rows, size), BF16),
            pltpu.VMEM((size, width), BF16),
            pltpu.VMEM(cache.shape, BF16),
            pltpu.VMEM(value_up.shape, BF16),
            pltpu.SemaphoreType.DMA((STEPS + 1 + parts,)),
        ],
        compiler_params=pltpu.CompilerParams(vmem_limit_bytes=60 << 20),
        cost_estimate=pl.CostEstimate(
            flops=4 * rows * heads * positions * depth * GROUP + 2 * rows * size * width,
            bytes_accessed=2 * rows * positions * depth + 2 * size * width,
            transcendentals=rows * heads * positions,
        ),
    )(lengths, query, cache, query_rope, cache_rope, value_up, out_proj.reshape(size, width))


OWNED = 4
SLAB = 2048
INNER = 2


def fetch(source, target, sem):
    copy = pltpu.make_async_copy(source, target, sem)
    copy.start()
    return copy


def front_kernel(planes, sides, *refs):
    blocks, refs = refs[:planes], refs[planes:]
    weights, refs = refs[: 2 * sides], refs[2 * sides :]
    gate, up, x, gate_w, up_w, row_sem, weight_sem = refs
    depth = x.shape[1]
    block = gate.shape[1]
    tile = depth // INNER
    half = gate_w.shape[1] // sides
    waits = []
    for at in range(INNER):
        here = pl.ds(at * tile, tile)
        copies = []
        for i, source in enumerate(weights):
            target = (gate_w, up_w)[i % 2].at[here, pl.ds(i // 2 * half, half)]
            copies.append(fetch(source.at[0, here], target, weight_sem.at[at, i]))
        for i, ref in enumerate(blocks):
            target = x.at[pl.ds(i * block, block), here]
            copies.append(fetch(ref.at[:, here], target, row_sem.at[at, i]))
        waits.append(copies)
    for at in range(INNER):
        for copy in waits[at]:
            copy.wait()
        here = slice(at * tile, (at + 1) * tile)
        gate_part = dot(x[:, here], gate_w[here]).reshape(gate.shape)
        up_part = dot(x[:, here], up_w[here]).reshape(up.shape)
        if at == 0:
            gate[...] = gate_part
            up[...] = up_part
        else:
            gate[...] += gate_part
            up[...] += up_part


def expert_front(blocks, weights):
    planes, sides = len(blocks), len(weights)
    block, depth = blocks[0].shape
    hidden = sides * weights[0][0].shape[2]
    wide = jax.ShapeDtypeStruct((planes, block, hidden), F32)
    anywhere = pl.BlockSpec(memory_space=pl.ANY)
    inside = pl.BlockSpec(memory_space=pltpu.VMEM)
    return pl.pallas_call(
        lambda *refs: front_kernel(planes, sides, *refs),
        out_shape=[wide, wide],
        in_specs=[anywhere] * (planes + 2 * sides),
        out_specs=[inside, inside],
        scratch_shapes=[
            pltpu.VMEM((planes * block, depth), BF16),
            pltpu.VMEM((depth, hidden), BF16),
            pltpu.VMEM((depth, hidden), BF16),
            pltpu.SemaphoreType.DMA((INNER, planes)),
            pltpu.SemaphoreType.DMA((INNER, 2 * sides)),
        ],
        compiler_params=pltpu.CompilerParams(vmem_limit_bytes=60 << 20),
        cost_estimate=pl.CostEstimate(
            flops=4 * planes * block * depth * hidden,
            bytes_accessed=2 * planes * block * depth + 4 * depth * hidden,
            transcendentals=0,
        ),
    )(*blocks, *[v for side in weights for v in side[:2]])


def expert_kernel(planes, sides, *refs):
    gate_ring, up_ring, mine, refs = refs[0], refs[1], refs[2], refs[3:]
    weights = [refs[3 * side : 3 * side + 3] for side in range(sides)]
    refs = refs[3 * sides :]
    outs, refs = refs[: planes + 1], refs[planes + 1 :]
    x, gate_w, up_w, down_w, *refs = refs
    gate_rest, up_rest, gate, up, spread, share_ring, share_rest = refs[:-3]
    row_sem, weight_sem, sent = refs[-3:]
    rest = x.shape[1]
    depth = weights[0][0].shape[1] - rest
    block = gate.shape[1]
    own = block // OWNED
    tile = rest // INNER
    size = share_ring.shape[1]
    half = gate_w.shape[1] // sides

    waits = []
    for at in range(INNER):
        copies = []
        here = pl.ds(at * tile, tile)
        for side in range(sides):
            columns = pl.ds(side * half, half)
            for i, target in enumerate((gate_w, up_w)):
                source = weights[side][i].at[0, pl.ds(depth + at * tile, tile)]
                copies.append(
                    fetch(source, target.at[here, columns], weight_sem.at[at, 2 * side + i])
                )
        copies.append(fetch(mine.at[:, here], x.at[:, here], row_sem.at[at]))
        waits.append(copies)
    ring_waits = [
        fetch(gate_ring, gate, row_sem.at[INNER]),
        fetch(up_ring, up, row_sem.at[INNER + 1]),
    ]
    down_waits = [
        fetch(weights[side][2].at[0], down_w.at[pl.ds(side * half, half)], weight_sem.at[INNER, side])
        for side in range(sides)
    ]

    for at in range(INNER):
        for copy in waits[at]:
            copy.wait()
        here = slice(at * tile, (at + 1) * tile)
        gate_part = dot(x[:, here], gate_w[here])
        up_part = dot(x[:, here], up_w[here])
        if at == 0:
            gate_rest[...] = gate_part
            up_rest[...] = up_part
        else:
            gate_rest[...] += gate_part
            up_rest[...] += up_part
    for copy in ring_waits:
        copy.wait()
    for turn in range(planes):
        for f in range(own):
            start = (f * planes + turn) * OWNED
            target = slice(f * OWNED, (f + 1) * OWNED)
            gate[turn, target] += gate_rest[start : start + OWNED]
            up[turn, target] += up_rest[start : start + OWNED]
    gated = gate[...]
    hidden = gated * jax.nn.sigmoid(gated) * up[...]
    gate[...] = hidden
    for copy in down_waits:
        copy.wait()
    hidden = hidden.reshape(planes * block, gate.shape[2]).astype(BF16)
    sends = []
    for at in range(0, size, SLAB):
        columns = slice(at, min(at + SLAB, size))
        share_ring[:, columns] = dot(hidden, down_w[:, columns]).astype(BF16)
    for turn in range(planes):
        piece = share_ring.at[pl.ds(turn * block, block)]
        sends.append(fetch(piece, outs[turn], sent.at[turn]))
        for f in range(own):
            start = (f * planes + turn) * OWNED
            spread[start : start + OWNED] = gate[turn, f * OWNED : (f + 1) * OWNED]
    share_rest[...] = dot(spread[...].astype(BF16), down_w[:, size:]).astype(BF16)
    sends.append(fetch(share_rest, outs[planes], sent.at[planes]))
    for copy in sends:
        copy.wait()


def expert(gate_ring, up_ring, mine, weights, size):
    planes, block, hidden = gate_ring.shape
    sides = len(weights)
    count, rest = mine.shape
    width = weights[0][2].shape[2]
    wide = (planes, block, hidden)
    anywhere = pl.BlockSpec(memory_space=pl.ANY)
    return pl.pallas_call(
        lambda *refs: expert_kernel(planes, sides, *refs),
        out_shape=[jax.ShapeDtypeStruct((block, size), BF16)] * planes
        + [jax.ShapeDtypeStruct((count, width - size), BF16)],
        in_specs=[anywhere] * (3 + 3 * sides),
        out_specs=[anywhere] * (planes + 1),
        scratch_shapes=[
            pltpu.VMEM((count, rest), BF16),
            pltpu.VMEM((rest, hidden), BF16),
            pltpu.VMEM((rest, hidden), BF16),
            pltpu.VMEM((hidden, width), BF16),
            pltpu.VMEM((count, hidden), F32),
            pltpu.VMEM((count, hidden), F32),
            pltpu.VMEM(wide, F32),
            pltpu.VMEM(wide, F32),
            pltpu.VMEM((count, hidden), F32),
            pltpu.VMEM((count, size), BF16),
            pltpu.VMEM((count, width - size), BF16),
            pltpu.SemaphoreType.DMA((INNER + 2,)),
            pltpu.SemaphoreType.DMA((INNER + 1, 2 * sides)),
            pltpu.SemaphoreType.DMA((planes + 1,)),
        ],
        compiler_params=pltpu.CompilerParams(vmem_limit_bytes=60 << 20),
        cost_estimate=pl.CostEstimate(
            flops=4 * count * rest * hidden + 2 * count * width * hidden,
            bytes_accessed=2 * count * (width + rest) + (4 * rest + 2 * width) * hidden,
            transcendentals=count * hidden,
        ),
    )(gate_ring, up_ring, mine, *[v for side in weights for v in side])


def local(
    query_latent,
    query_rope,
    cache_latent,
    cache_rope,
    lengths,
    value_up,
    out_proj,
    residual,
    norm_gain,
    expert_ids,
    route_weights,
    gate_proj,
    up_proj,
    down_proj,
):
    row_count, width = residual.shape
    owners = lax.axis_size("ffn")
    cores = 2
    planes = lax.axis_size("attn") // cores
    swap = [(a, a ^ 1) for a in range(planes * cores)]

    def from_plane(v, ahead):
        pairs = [
            (((y + ahead) % planes) * cores + c, y * cores + c)
            for y in range(planes)
            for c in range(cores)
        ]
        return lax.ppermute(v, "attn", pairs)

    def along_planes(v):
        return jnp.stack([v] + [from_plane(v, ahead) for ahead in range(1, planes)])

    named = expert_ids[:, :, None] == jnp.arange(owners, dtype=jnp.int32)[None, None, :]
    routed = jnp.sum(named.astype(F32), axis=1)
    row_weights = jnp.sum(jnp.where(named, route_weights[:, :, None], F32(0.0)), axis=1)
    capacity = min(row_count, row_count * expert_ids.shape[1] // owners + 1)

    def slots_of(routed, weight):
        rank = jnp.cumsum(routed, axis=-2) - routed
        routed, weight, rank = (jnp.moveaxis(v, -1, 0)[..., None, :] for v in (routed, weight, rank))
        slot = jnp.arange(capacity, dtype=jnp.int32).astype(F32)[:, None]
        placed = ((routed == 1.0) & (rank == slot)).astype(F32)
        return placed, placed * weight

    score_scale = (value_up.shape[2] + query_rope.shape[2]) ** (-0.5)
    pieces = attend(
        query_latent,
        query_rope,
        cache_latent,
        cache_rope,
        lengths,
        value_up,
        out_proj,
        score_scale,
        owners,
        PARTS,
    )
    eye = jnp.eye(planes, dtype=F32)

    def block_diagonal(v):
        spread = v[:, :, :, None, :] * eye[None, :, None, :, None]
        return spread.reshape(owners * planes * capacity, planes * row_count)

    placed, weighting = slots_of(routed, row_weights)
    placed = placed.reshape(owners * capacity, row_count).astype(BF16)
    weighting = weighting.reshape(owners * capacity, row_count)
    terms, left = [routed], row_weights
    for _ in range(3):
        term = lax.reduce_precision(left, 8, 7)
        terms.append(term)
        left = left - term
    table = jnp.pad(jnp.concatenate(terms, axis=1), ((0, 0), (0, 128 - 4 * owners))).astype(BF16)
    pieces = lax.all_to_all(pieces, "ffn", split_axis=0, concat_axis=0, tiled=True)
    weights_here = (gate_proj, up_proj, down_proj)
    weights_there = [lax.ppermute(v, "attn", swap) for v in weights_here]
    pieces, weights_there = lax.optimization_barrier((pieces, weights_there))
    attended = (
        jnp.sum(pieces.astype(F32), axis=0)
        .reshape(PARTS, row_count, width // PARTS)
        .transpose(1, 0, 2)
        .reshape(row_count, width)
    )
    mixed = residual.astype(F32) + attended
    inverse = lax.rsqrt(jnp.mean(mixed * mixed, axis=1, keepdims=True) + 1e-06)
    normed = (mixed * inverse * norm_gain.astype(F32)[None, :]).astype(BF16)

    outgoing = dot(placed, normed[:, :IN_RING]).astype(BF16).reshape(owners, capacity, IN_RING)
    near = jnp.concatenate([normed[:, IN_RING:], table], axis=1)
    arrived = lax.all_to_all(outgoing, "ffn", split_axis=0, concat_axis=0, tiled=True)
    arrived = arrived.reshape(owners * capacity, IN_RING)

    rest = width - IN_RING
    by_plane = [arrived] + [from_plane(arrived, ahead) for ahead in range(1, planes)]
    near = along_planes(near)
    tables = near[:, :, rest:].astype(F32)
    tables = [tables[:, :, at * owners : (at + 1) * owners] for at in range(4)]
    placed_all, weighting_all = slots_of(tables[0], tables[1] + tables[2] + tables[3])
    placed_all = block_diagonal(placed_all).astype(BF16)
    weighting_all = block_diagonal(weighting_all)
    near = near[:, :, :rest].reshape(planes * row_count, rest)
    outgoing = dot(placed_all, near).astype(BF16).reshape(owners, planes * capacity, rest)
    mine = lax.all_to_all(outgoing, "ffn", split_axis=0, concat_axis=0, tiled=True)
    weights = (weights_here, weights_there)
    gate_ring, up_ring = expert_front(by_plane, weights)
    gate_ring, up_ring, mine = lax.optimization_barrier((gate_ring, up_ring, mine))
    mine = mine.reshape(owners * planes * capacity, rest)
    *ring, ours = expert(gate_ring, up_ring, mine, weights, OUT_RING)

    summed = ring[0].astype(F32)
    for ahead in range(1, planes):
        summed = summed + from_plane(ring[planes - ahead], ahead).astype(F32)
    summed = summed.astype(BF16)

    rest = width - OUT_RING
    ours = ours.reshape(owners, planes * capacity, rest)
    ours = lax.all_to_all(ours, "ffn", split_axis=0, concat_axis=0, tiled=True)
    ours = jnp.einsum(
        "sr,sd->rd",
        weighting_all,
        ours.reshape(owners * planes * capacity, rest).astype(F32),
        precision=lax.Precision.HIGHEST,
    ).astype(BF16)
    ours = ours.reshape(planes, row_count, rest)
    sum_rest = ours[0].astype(F32)
    for ahead in range(1, planes):
        sum_rest = sum_rest + from_plane(ours[planes - ahead], ahead).astype(F32)

    returned = lax.all_to_all(
        summed.reshape(owners, capacity, OUT_RING), "ffn", split_axis=0, concat_axis=0, tiled=True
    )
    sum_ring = jnp.einsum(
        "sr,sd->rd",
        weighting,
        returned.reshape(owners * capacity, OUT_RING).astype(F32),
        precision=lax.Precision.HIGHEST,
    )
    return (mixed + jnp.concatenate([sum_ring, sum_rest], axis=1)).astype(BF16)


def solution(mesh):
    return jax.shard_map(
        local,
        mesh=mesh,
        in_specs=(
            P("attn", "ffn", None),
            P("attn", "ffn", None),
            P("attn", None, None),
            P("attn", None, None),
            P("attn"),
            P("ffn", None, None),
            P("ffn", None, None),
            P(("attn", "ffn"), None),
            P(),
            P(("attn", "ffn"), None),
            P(("attn", "ffn"), None),
            P("ffn", None, "attn"),
            P("ffn", None, "attn"),
            P("ffn", "attn", None),
        ),
        out_specs=P(("attn", "ffn"), None),
        check_vma=False,
    )
```

```python
import math

import jax
import jax.numpy as jnp
from jax import lax
from jax.experimental import pallas as pl
from jax.experimental.pallas import tpu as pltpu
from jax.sharding import PartitionSpec as P

PARTS = 4
UNIT = 512
IN_RING = 3072
OUT_RING = 4096
F32 = jnp.float32
BF16 = jnp.bfloat16


def dot(a, b):
    return jnp.dot(a, b, preferred_element_type=F32)


GROUP = 4
STEPS = 3

def attend_kernel(
    scale,
    owners,
    parts,
    lengths,
    query,
    cache_here,
    query_rope,
    cache_rope,
    value_here,
    out_proj,
    out,
    rope,
    latent,
    values,
    weights,
    cache,
    value_up,
    arrived,
):
    all_rows, heads, depth = query.shape
    positions = cache.shape[1]
    rows = all_rows // STEPS
    count = GROUP * heads
    width = weights.shape[1] // parts

    def fetch(source, target, at):
        copy = pltpu.make_async_copy(source, target, arrived.at[at])
        copy.start()
        return copy

    chunks = []
    for step in range(STEPS):
        here = pl.ds(step * rows, rows)
        chunks.append(fetch(cache_here.at[here], cache.at[here], step))
    value_fetch = fetch(value_here, value_up, STEPS)
    fetches = []
    for part in range(parts):
        columns = pl.ds(part * width, width)
        fetches.append(
            fetch(out_proj.at[:, columns], weights.at[:, columns], STEPS + 1 + part)
        )

    for h in range(heads):
        vector = query_rope[h].astype(F32)
        terms = []
        for at in range(positions):
            terms.append(jnp.sum(vector * cache_rope[at].astype(F32), axis=0, keepdims=True))
        wide = jnp.concatenate(terms, axis=0).T
        rope[pl.ds(h, all_rows, heads), :] = jnp.concatenate([wide] * 2, axis=1)

    groups = rows // GROUP
    total = rows * heads
    for step in range(STEPS):
        chunks[step].wait()
        first = step * rows
        base = step * total
        keys = [
            cache[first + group * GROUP : first + (group + 1) * GROUP].reshape(
                GROUP * positions, depth
            )
            for group in range(groups)
        ]
        scores = []
        for group in range(groups):
            queries = jnp.concatenate(
                [query[first + group * GROUP + i] for i in range(GROUP)], axis=0
            )
            scores.append(
                lax.dot_general(
                    queries, keys[group], (((1,), (1,)), ((), ())), preferred_element_type=F32
                )
            )
        scores = jnp.concatenate(scores, axis=0)
        near = rope[base : base + total, :]
        scores = (scores + jnp.concatenate([near] * (GROUP // 2), axis=1)) * scale
        row = lax.broadcasted_iota(jnp.int32, scores.shape, 0) // heads
        own = lax.broadcasted_iota(jnp.int32, scores.shape, 1) - (row % GROUP) * positions
        limit = jnp.concatenate(
            [
                jnp.full((heads, GROUP * positions), lengths[first + i], jnp.int32)
                for i in range(rows)
            ],
            axis=0,
        )
        live = (own >= 0) & (own < limit)
        scores = jnp.where(live, scores, F32(-1e30))
        top = jnp.max(scores, axis=1, keepdims=True)
        expo = jnp.where(live, jnp.exp(scores - top), F32(0.0))
        probs = (expo / jnp.sum(expo, axis=1, keepdims=True)).astype(BF16)
        mixed = jnp.concatenate(
            [
                dot(probs[group * count : (group + 1) * count], keys[group])
                for group in range(groups)
            ],
            axis=0,
        )
        for part in range(depth // 128):
            latent[part, base : base + total, :] = mixed[:, part * 128 : (part + 1) * 128]

    value_fetch.wait()
    size = value_up.shape[2]
    for h in range(heads):
        mixed = jnp.concatenate(
            [latent[part, pl.ds(h, all_rows, heads), :] for part in range(depth // 128)], axis=1
        ).astype(BF16)
        values[:, h * size : (h + 1) * size] = dot(mixed, value_up[h]).astype(BF16)
    own_rows = all_rows // owners
    for part, copy in enumerate(fetches):
        copy.wait()
        result = dot(values[...], weights[:, part * width : (part + 1) * width]).astype(BF16)
        for f in range(owners):
            out[f, part * own_rows : (part + 1) * own_rows] = result[
                f * own_rows : (f + 1) * own_rows
            ]


def attend(query, query_rope, cache, cache_rope, lengths, value_up, out_proj, scale, owners, parts):
    rows, heads, depth = query.shape
    positions = cache.shape[1]
    size = heads * value_up.shape[2]
    width = out_proj.shape[2]
    shape = (owners, parts * (rows // owners), width // parts)
    anywhere = pl.BlockSpec(memory_space=pl.ANY)
    inside = pl.BlockSpec(memory_space=pltpu.VMEM)
    query_rope = jnp.transpose(query_rope, (1, 2, 0))
    cache_rope = jnp.transpose(cache_rope, (1, 2, 0))
    return pl.pallas_call(
        lambda *refs: attend_kernel(scale, owners, parts, *refs),
        out_shape=jax.ShapeDtypeStruct(shape, BF16),
        in_specs=[
            pl.BlockSpec(memory_space=pltpu.SMEM),
            inside,
            anywhere,
            inside,
            inside,
            anywhere,
            anywhere,
        ],
        out_specs=inside,
        scratch_shapes=[
            pltpu.VMEM((rows * heads, 2 * positions), F32),
            pltpu.VMEM((depth // 128, rows * heads, 128), F32),
            pltpu.VMEM((rows, size), BF16),
            pltpu.VMEM((size, width), BF16),
            pltpu.VMEM(cache.shape, BF16),
            pltpu.VMEM(value_up.shape, BF16),
            pltpu.SemaphoreType.DMA((STEPS + 1 + parts,)),
        ],
        compiler_params=pltpu.CompilerParams(vmem_limit_bytes=62 << 20),
        cost_estimate=pl.CostEstimate(
            flops=4 * rows * heads * positions * depth * GROUP + 2 * rows * size * width,
            bytes_accessed=2 * rows * positions * depth + 2 * size * width,
            transcendentals=rows * heads * positions,
        ),
    )(lengths, query, cache, query_rope, cache_rope, value_up, out_proj.reshape(size, width))


OWNED = 4
SLAB = 2048
INNER = 2


def fetch(source, target, sem):
    copy = pltpu.make_async_copy(source, target, sem)
    copy.start()
    return copy


def front_kernel(planes, sides, *refs):
    blocks, refs = refs[:planes], refs[planes:]
    weights, refs = refs[: 2 * sides], refs[2 * sides :]
    gate, up, x, gate_w, up_w, row_sem, weight_sem = refs
    depth = x.shape[1]
    block = gate.shape[1]
    tile = depth // INNER
    half = gate_w.shape[1] // sides
    waits = []
    for at in range(INNER):
        here = pl.ds(at * tile, tile)
        copies = []
        for i, source in enumerate(weights):
            target = (gate_w, up_w)[i % 2].at[here, pl.ds(i // 2 * half, half)]
            copies.append(fetch(source.at[0, here], target, weight_sem.at[at, i]))
        for i, ref in enumerate(blocks):
            target = x.at[pl.ds(i * block, block), here]
            copies.append(fetch(ref.at[:, here], target, row_sem.at[at, i]))
        waits.append(copies)
    for at in range(INNER):
        for copy in waits[at]:
            copy.wait()
        here = slice(at * tile, (at + 1) * tile)
        gate_part = dot(x[:, here], gate_w[here]).reshape(gate.shape)
        up_part = dot(x[:, here], up_w[here]).reshape(up.shape)
        if at == 0:
            gate[...] = gate_part
            up[...] = up_part
        else:
            gate[...] += gate_part
            up[...] += up_part


def expert_front(blocks, weights):
    planes, sides = len(blocks), len(weights)
    block, depth = blocks[0].shape
    hidden = sides * weights[0][0].shape[2]
    wide = jax.ShapeDtypeStruct((planes, block, hidden), F32)
    anywhere = pl.BlockSpec(memory_space=pl.ANY)
    inside = pl.BlockSpec(memory_space=pltpu.VMEM)
    return pl.pallas_call(
        lambda *refs: front_kernel(planes, sides, *refs),
        out_shape=[wide, wide],
        in_specs=[anywhere] * (planes + 2 * sides),
        out_specs=[inside, inside],
        scratch_shapes=[
            pltpu.VMEM((planes * block, depth), BF16),
            pltpu.VMEM((depth, hidden), BF16),
            pltpu.VMEM((depth, hidden), BF16),
            pltpu.SemaphoreType.DMA((INNER, planes)),
            pltpu.SemaphoreType.DMA((INNER, 2 * sides)),
        ],
        compiler_params=pltpu.CompilerParams(vmem_limit_bytes=62 << 20),
        cost_estimate=pl.CostEstimate(
            flops=4 * planes * block * depth * hidden,
            bytes_accessed=2 * planes * block * depth + 4 * depth * hidden,
            transcendentals=0,
        ),
    )(*blocks, *[v for side in weights for v in side[:2]])


def expert_kernel(planes, sides, *refs):
    gate_ring, up_ring, mine, refs = refs[0], refs[1], refs[2], refs[3:]
    weights = [refs[3 * side : 3 * side + 3] for side in range(sides)]
    refs = refs[3 * sides :]
    outs, refs = refs[: planes + 1], refs[planes + 1 :]
    x, gate_w, up_w, down_w, *refs = refs
    gate_rest, up_rest, gate, up, spread, share_ring, share_rest = refs[:-3]
    row_sem, weight_sem, sent = refs[-3:]
    rest = x.shape[1]
    depth = weights[0][0].shape[1] - rest
    block = gate.shape[1]
    own = block // OWNED
    tile = rest // INNER
    size = share_ring.shape[1]
    half = gate_w.shape[1] // sides

    waits = []
    for at in range(INNER):
        copies = []
        here = pl.ds(at * tile, tile)
        for side in range(sides):
            columns = pl.ds(side * half, half)
            for i, target in enumerate((gate_w, up_w)):
                source = weights[side][i].at[0, pl.ds(depth + at * tile, tile)]
                copies.append(
                    fetch(source, target.at[here, columns], weight_sem.at[at, 2 * side + i])
                )
        copies.append(fetch(mine.at[:, here], x.at[:, here], row_sem.at[at]))
        waits.append(copies)
    ring_waits = [
        fetch(gate_ring, gate, row_sem.at[INNER]),
        fetch(up_ring, up, row_sem.at[INNER + 1]),
    ]
    down_waits = [
        fetch(weights[side][2].at[0], down_w.at[pl.ds(side * half, half)], weight_sem.at[INNER, side])
        for side in range(sides)
    ]

    for at in range(INNER):
        for copy in waits[at]:
            copy.wait()
        here = slice(at * tile, (at + 1) * tile)
        gate_part = dot(x[:, here], gate_w[here])
        up_part = dot(x[:, here], up_w[here])
        if at == 0:
            gate_rest[...] = gate_part
            up_rest[...] = up_part
        else:
            gate_rest[...] += gate_part
            up_rest[...] += up_part
    for copy in ring_waits:
        copy.wait()
    for turn in range(planes):
        for f in range(own):
            start = (f * planes + turn) * OWNED
            target = slice(f * OWNED, (f + 1) * OWNED)
            gate[turn, target] += gate_rest[start : start + OWNED]
            up[turn, target] += up_rest[start : start + OWNED]
    gated = gate[...]
    hidden = gated * jax.nn.sigmoid(gated) * up[...]
    gate[...] = hidden
    for copy in down_waits:
        copy.wait()
    hidden = hidden.reshape(planes * block, gate.shape[2]).astype(BF16)
    sends = []
    for at in range(0, size, SLAB):
        columns = slice(at, min(at + SLAB, size))
        share_ring[:, columns] = dot(hidden, down_w[:, columns]).astype(BF16)
    for turn in range(planes):
        piece = share_ring.at[pl.ds(turn * block, block)]
        sends.append(fetch(piece, outs[turn], sent.at[turn]))
        for f in range(own):
            start = (f * planes + turn) * OWNED
            spread[start : start + OWNED] = gate[turn, f * OWNED : (f + 1) * OWNED]
    share_rest[...] = dot(spread[...].astype(BF16), down_w[:, size:]).astype(BF16)
    sends.append(fetch(share_rest, outs[planes], sent.at[planes]))
    for copy in sends:
        copy.wait()


def expert(gate_ring, up_ring, mine, weights, size):
    planes, block, hidden = gate_ring.shape
    sides = len(weights)
    count, rest = mine.shape
    width = weights[0][2].shape[2]
    wide = (planes, block, hidden)
    anywhere = pl.BlockSpec(memory_space=pl.ANY)
    return pl.pallas_call(
        lambda *refs: expert_kernel(planes, sides, *refs),
        out_shape=[jax.ShapeDtypeStruct((block, size), BF16)] * planes
        + [jax.ShapeDtypeStruct((count, width - size), BF16)],
        in_specs=[anywhere] * (3 + 3 * sides),
        out_specs=[anywhere] * (planes + 1),
        scratch_shapes=[
            pltpu.VMEM((count, rest), BF16),
            pltpu.VMEM((rest, hidden), BF16),
            pltpu.VMEM((rest, hidden), BF16),
            pltpu.VMEM((hidden, width), BF16),
            pltpu.VMEM((count, hidden), F32),
            pltpu.VMEM((count, hidden), F32),
            pltpu.VMEM(wide, F32),
            pltpu.VMEM(wide, F32),
            pltpu.VMEM((count, hidden), F32),
            pltpu.VMEM((count, size), BF16),
            pltpu.VMEM((count, width - size), BF16),
            pltpu.SemaphoreType.DMA((INNER + 2,)),
            pltpu.SemaphoreType.DMA((INNER + 1, 2 * sides)),
            pltpu.SemaphoreType.DMA((planes + 1,)),
        ],
        compiler_params=pltpu.CompilerParams(vmem_limit_bytes=62 << 20),
        cost_estimate=pl.CostEstimate(
            flops=4 * count * rest * hidden + 2 * count * width * hidden,
            bytes_accessed=2 * count * (width + rest) + (4 * rest + 2 * width) * hidden,
            transcendentals=count * hidden,
        ),
    )(gate_ring, up_ring, mine, *[v for side in weights for v in side])


def local(
    query_latent,
    query_rope,
    cache_latent,
    cache_rope,
    lengths,
    value_up,
    out_proj,
    residual,
    norm_gain,
    expert_ids,
    route_weights,
    gate_proj,
    up_proj,
    down_proj,
):
    row_count, width = residual.shape
    owners = lax.axis_size("ffn")
    cores = 2
    planes = lax.axis_size("attn") // cores
    swap = [(a, a ^ 1) for a in range(planes * cores)]

    def from_plane(v, ahead):
        pairs = [
            (((y + ahead) % planes) * cores + c, y * cores + c)
            for y in range(planes)
            for c in range(cores)
        ]
        return lax.ppermute(v, "attn", pairs)

    def along_planes(v):
        return jnp.stack([v] + [from_plane(v, ahead) for ahead in range(1, planes)])

    named = expert_ids[:, :, None] == jnp.arange(owners, dtype=jnp.int32)[None, None, :]
    routed = jnp.sum(named.astype(F32), axis=1)
    row_weights = jnp.sum(jnp.where(named, route_weights[:, :, None], F32(0.0)), axis=1)
    capacity = min(row_count, row_count * expert_ids.shape[1] // owners + 1)

    def slots_of(routed, weight):
        rank = jnp.cumsum(routed, axis=-2) - routed
        routed, weight, rank = (jnp.moveaxis(v, -1, 0)[..., None, :] for v in (routed, weight, rank))
        slot = jnp.arange(capacity, dtype=jnp.int32).astype(F32)[:, None]
        placed = ((routed == 1.0) & (rank == slot)).astype(F32)
        return placed, placed * weight

    score_scale = (value_up.shape[2] + query_rope.shape[2]) ** (-0.5)
    pieces = attend(
        query_latent,
        query_rope,
        cache_latent,
        cache_rope,
        lengths,
        value_up,
        out_proj,
        score_scale,
        owners,
        PARTS,
    )
    eye = jnp.eye(planes, dtype=F32)

    def block_diagonal(v):
        spread = v[:, :, :, None, :] * eye[None, :, None, :, None]
        return spread.reshape(owners * planes * capacity, planes * row_count)

    placed, weighting = slots_of(routed, row_weights)
    placed = placed.reshape(owners * capacity, row_count).astype(BF16)
    weighting = weighting.reshape(owners * capacity, row_count)
    terms, left = [routed], row_weights
    for _ in range(3):
        term = lax.reduce_precision(left, 8, 7)
        terms.append(term)
        left = left - term
    table = jnp.pad(jnp.concatenate(terms, axis=1), ((0, 0), (0, 128 - 4 * owners))).astype(BF16)
    pieces = lax.all_to_all(pieces, "ffn", split_axis=0, concat_axis=0, tiled=True)
    weights_here = (gate_proj, up_proj, down_proj)
    weights_there = [lax.ppermute(v, "attn", swap) for v in weights_here]
    pieces, weights_there = lax.optimization_barrier((pieces, weights_there))
    attended = (
        jnp.sum(pieces.astype(F32), axis=0)
        .reshape(PARTS, row_count, width // PARTS)
        .transpose(1, 0, 2)
        .reshape(row_count, width)
    )
    mixed = residual.astype(F32) + attended
    inverse = lax.rsqrt(jnp.mean(mixed * mixed, axis=1, keepdims=True) + 1e-06)
    normed = (mixed * inverse * norm_gain.astype(F32)[None, :]).astype(BF16)

    outgoing = dot(placed, normed[:, :IN_RING]).astype(BF16).reshape(owners, capacity, IN_RING)
    near = jnp.concatenate([normed[:, IN_RING:], table], axis=1)
    arrived = lax.all_to_all(outgoing, "ffn", split_axis=0, concat_axis=0, tiled=True)
    arrived = arrived.reshape(owners * capacity, IN_RING)

    rest = width - IN_RING
    by_plane = [arrived] + [from_plane(arrived, ahead) for ahead in range(1, planes)]
    near = along_planes(near)
    tables = near[:, :, rest:].astype(F32)
    tables = [tables[:, :, at * owners : (at + 1) * owners] for at in range(4)]
    placed_all, weighting_all = slots_of(tables[0], tables[1] + tables[2] + tables[3])
    placed_all = block_diagonal(placed_all).astype(BF16)
    weighting_all = block_diagonal(weighting_all)
    near = near[:, :, :rest].reshape(planes * row_count, rest)
    outgoing = dot(placed_all, near).astype(BF16).reshape(owners, planes * capacity, rest)
    mine = lax.all_to_all(outgoing, "ffn", split_axis=0, concat_axis=0, tiled=True)
    weights = (weights_here, weights_there)
    gate_ring, up_ring = expert_front(by_plane, weights)
    gate_ring, up_ring, mine = lax.optimization_barrier((gate_ring, up_ring, mine))
    mine = mine.reshape(owners * planes * capacity, rest)
    *ring, ours = expert(gate_ring, up_ring, mine, weights, OUT_RING)

    summed = ring[0].astype(F32)
    for ahead in range(1, planes):
        summed = summed + from_plane(ring[planes - ahead], ahead).astype(F32)
    summed = summed.astype(BF16)

    rest = width - OUT_RING
    ours = ours.reshape(owners, planes * capacity, rest)
    ours = lax.all_to_all(ours, "ffn", split_axis=0, concat_axis=0, tiled=True)
    ours = jnp.einsum(
        "sr,sd->rd",
        weighting_all,
        ours.reshape(owners * planes * capacity, rest).astype(F32),
        precision=lax.Precision.HIGHEST,
    ).astype(BF16)
    ours = ours.reshape(planes, row_count, rest)
    sum_rest = ours[0].astype(F32)
    for ahead in range(1, planes):
        sum_rest = sum_rest + from_plane(ours[planes - ahead], ahead).astype(F32)

    returned = lax.all_to_all(
        summed.reshape(owners, capacity, OUT_RING), "ffn", split_axis=0, concat_axis=0, tiled=True
    )
    sum_ring = jnp.einsum(
        "sr,sd->rd",
        weighting,
        returned.reshape(owners * capacity, OUT_RING).astype(F32),
        precision=lax.Precision.HIGHEST,
    )
    return (mixed + jnp.concatenate([sum_ring, sum_rest], axis=1)).astype(BF16)


def solution(mesh):
    return jax.shard_map(
        local,
        mesh=mesh,
        in_specs=(
            P("attn", "ffn", None),
            P("attn", "ffn", None),
            P("attn", None, None),
            P("attn", None, None),
            P("attn"),
            P("ffn", None, None),
            P("ffn", None, None),
            P(("attn", "ffn"), None),
            P(),
            P(("attn", "ffn"), None),
            P(("attn", "ffn"), None),
            P("ffn", None, "attn"),
            P("ffn", None, "attn"),
            P("ffn", "attn", None),
        ),
        out_specs=P(("attn", "ffn"), None),
        check_vma=False,
    )
```

```python
import math

import jax
import jax.numpy as jnp
from jax import lax
from jax.experimental import pallas as pl
from jax.experimental.pallas import tpu as pltpu
from jax.sharding import PartitionSpec as P

PARTS = 4
UNIT = 512
IN_RING = 3072
OUT_RING = 4096
F32 = jnp.float32
BF16 = jnp.bfloat16


def dot(a, b):
    return jnp.dot(a, b, preferred_element_type=F32)


GROUP = 4
STEPS = 3

def attend_kernel(
    scale,
    owners,
    parts,
    lengths,
    query,
    cache_here,
    query_rope,
    cache_rope,
    value_here,
    out_proj,
    out,
    rope,
    latent,
    values,
    weights,
    cache,
    value_up,
    arrived,
):
    all_rows, heads, depth = query.shape
    positions = cache.shape[1]
    rows = all_rows // STEPS
    count = GROUP * heads
    width = weights.shape[1] // parts

    def fetch(source, target, at):
        copy = pltpu.make_async_copy(source, target, arrived.at[at])
        copy.start()
        return copy

    chunks = []
    for step in range(STEPS):
        here = pl.ds(step * rows, rows)
        chunks.append(fetch(cache_here.at[here], cache.at[here], step))
    value_fetch = fetch(value_here, value_up, STEPS)
    fetches = []
    for part in range(parts):
        columns = pl.ds(part * width, width)
        fetches.append(
            fetch(out_proj.at[:, columns], weights.at[:, columns], STEPS + 1 + part)
        )

    for h in range(heads):
        vector = query_rope[h].astype(F32)
        terms = []
        for at in range(positions):
            terms.append(jnp.sum(vector * cache_rope[at].astype(F32), axis=0, keepdims=True))
        wide = jnp.concatenate(terms, axis=0).T
        rope[pl.ds(h, all_rows, heads), :] = jnp.concatenate([wide] * 2, axis=1)

    groups = rows // GROUP
    total = rows * heads
    for step in range(STEPS):
        chunks[step].wait()
        first = step * rows
        base = step * total
        keys = [
            cache[first + group * GROUP : first + (group + 1) * GROUP].reshape(
                GROUP * positions, depth
            )
            for group in range(groups)
        ]
        scores = []
        for group in range(groups):
            queries = jnp.concatenate(
                [query[first + group * GROUP + i] for i in range(GROUP)], axis=0
            )
            scores.append(
                lax.dot_general(
                    queries, keys[group], (((1,), (1,)), ((), ())), preferred_element_type=F32
                )
            )
        scores = jnp.concatenate(scores, axis=0)
        near = rope[base : base + total, :]
        scores = (scores + jnp.concatenate([near] * (GROUP // 2), axis=1)) * scale
        row = lax.broadcasted_iota(jnp.int32, scores.shape, 0) // heads
        own = lax.broadcasted_iota(jnp.int32, scores.shape, 1) - (row % GROUP) * positions
        limit = jnp.concatenate(
            [
                jnp.full((heads, GROUP * positions), lengths[first + i], jnp.int32)
                for i in range(rows)
            ],
            axis=0,
        )
        live = (own >= 0) & (own < limit)
        scores = jnp.where(live, scores, F32(-1e30))
        top = jnp.max(scores, axis=1, keepdims=True)
        expo = jnp.where(live, jnp.exp(scores - top), F32(0.0))
        probs = (expo / jnp.sum(expo, axis=1, keepdims=True)).astype(BF16)
        mixed = jnp.concatenate(
            [
                dot(probs[group * count : (group + 1) * count], keys[group])
                for group in range(groups)
            ],
            axis=0,
        )
        for part in range(depth // 128):
            latent[part, base : base + total, :] = mixed[:, part * 128 : (part + 1) * 128]

    value_fetch.wait()
    size = value_up.shape[2]
    for h in range(heads):
        mixed = jnp.concatenate(
            [latent[part, pl.ds(h, all_rows, heads), :] for part in range(depth // 128)], axis=1
        ).astype(BF16)
        values[:, h * size : (h + 1) * size] = dot(mixed, value_up[h]).astype(BF16)
    own_rows = all_rows // owners
    for part, copy in enumerate(fetches):
        copy.wait()
        result = dot(values[...], weights[:, part * width : (part + 1) * width]).astype(BF16)
        for f in range(owners):
            out[f, part * own_rows : (part + 1) * own_rows] = result[
                f * own_rows : (f + 1) * own_rows
            ]


def attend(query, query_rope, cache, cache_rope, lengths, value_up, out_proj, scale, owners, parts):
    rows, heads, depth = query.shape
    positions = cache.shape[1]
    size = heads * value_up.shape[2]
    width = out_proj.shape[2]
    shape = (owners, parts * (rows // owners), width // parts)
    anywhere = pl.BlockSpec(memory_space=pl.ANY)
    inside = pl.BlockSpec(memory_space=pltpu.VMEM)
    query_rope = jnp.transpose(query_rope, (1, 2, 0))
    cache_rope = jnp.transpose(cache_rope, (1, 2, 0))
    return pl.pallas_call(
        lambda *refs: attend_kernel(scale, owners, parts, *refs),
        out_shape=jax.ShapeDtypeStruct(shape, BF16),
        in_specs=[
            pl.BlockSpec(memory_space=pltpu.SMEM),
            inside,
            anywhere,
            inside,
            inside,
            anywhere,
            anywhere,
        ],
        out_specs=inside,
        scratch_shapes=[
            pltpu.VMEM((rows * heads, 2 * positions), F32),
            pltpu.VMEM((depth // 128, rows * heads, 128), F32),
            pltpu.VMEM((rows, size), BF16),
            pltpu.VMEM((size, width), BF16),
            pltpu.VMEM(cache.shape, BF16),
            pltpu.VMEM(value_up.shape, BF16),
            pltpu.SemaphoreType.DMA((STEPS + 1 + parts,)),
        ],
        compiler_params=pltpu.CompilerParams(vmem_limit_bytes=63 << 20),
        cost_estimate=pl.CostEstimate(
            flops=4 * rows * heads * positions * depth * GROUP + 2 * rows * size * width,
            bytes_accessed=2 * rows * positions * depth + 2 * size * width,
            transcendentals=rows * heads * positions,
        ),
    )(lengths, query, cache, query_rope, cache_rope, value_up, out_proj.reshape(size, width))


OWNED = 4
SLAB = 2048
INNER = 2


def fetch(source, target, sem):
    copy = pltpu.make_async_copy(source, target, sem)
    copy.start()
    return copy


def front_kernel(planes, sides, *refs):
    blocks, refs = refs[:planes], refs[planes:]
    weights, refs = refs[: 2 * sides], refs[2 * sides :]
    gate, up, x, gate_w, up_w, row_sem, weight_sem = refs
    depth = x.shape[1]
    block = gate.shape[1]
    tile = depth // INNER
    half = gate_w.shape[1] // sides
    waits = []
    for at in range(INNER):
        here = pl.ds(at * tile, tile)
        copies = []
        for i, source in enumerate(weights):
            target = (gate_w, up_w)[i % 2].at[here, pl.ds(i // 2 * half, half)]
            copies.append(fetch(source.at[0, here], target, weight_sem.at[at, i]))
        for i, ref in enumerate(blocks):
            target = x.at[pl.ds(i * block, block), here]
            copies.append(fetch(ref.at[:, here], target, row_sem.at[at, i]))
        waits.append(copies)
    for at in range(INNER):
        for copy in waits[at]:
            copy.wait()
        here = slice(at * tile, (at + 1) * tile)
        gate_part = dot(x[:, here], gate_w[here]).reshape(gate.shape)
        up_part = dot(x[:, here], up_w[here]).reshape(up.shape)
        if at == 0:
            gate[...] = gate_part
            up[...] = up_part
        else:
            gate[...] += gate_part
            up[...] += up_part


def expert_front(blocks, weights):
    planes, sides = len(blocks), len(weights)
    block, depth = blocks[0].shape
    hidden = sides * weights[0][0].shape[2]
    wide = jax.ShapeDtypeStruct((planes, block, hidden), F32)
    anywhere = pl.BlockSpec(memory_space=pl.ANY)
    inside = pl.BlockSpec(memory_space=pltpu.VMEM)
    return pl.pallas_call(
        lambda *refs: front_kernel(planes, sides, *refs),
        out_shape=[wide, wide],
        in_specs=[anywhere] * (planes + 2 * sides),
        out_specs=[inside, inside],
        scratch_shapes=[
            pltpu.VMEM((planes * block, depth), BF16),
            pltpu.VMEM((depth, hidden), BF16),
            pltpu.VMEM((depth, hidden), BF16),
            pltpu.SemaphoreType.DMA((INNER, planes)),
            pltpu.SemaphoreType.DMA((INNER, 2 * sides)),
        ],
        compiler_params=pltpu.CompilerParams(vmem_limit_bytes=63 << 20),
        cost_estimate=pl.CostEstimate(
            flops=4 * planes * block * depth * hidden,
            bytes_accessed=2 * planes * block * depth + 4 * depth * hidden,
            transcendentals=0,
        ),
    )(*blocks, *[v for side in weights for v in side[:2]])


def expert_kernel(planes, sides, *refs):
    gate_ring, up_ring, mine, refs = refs[0], refs[1], refs[2], refs[3:]
    weights = [refs[3 * side : 3 * side + 3] for side in range(sides)]
    refs = refs[3 * sides :]
    outs, refs = refs[: planes + 1], refs[planes + 1 :]
    x, gate_w, up_w, down_w, *refs = refs
    gate_rest, up_rest, gate, up, spread, share_ring, share_rest = refs[:-3]
    row_sem, weight_sem, sent = refs[-3:]
    rest = x.shape[1]
    depth = weights[0][0].shape[1] - rest
    block = gate.shape[1]
    own = block // OWNED
    tile = rest // INNER
    size = share_ring.shape[1]
    half = gate_w.shape[1] // sides

    waits = []
    for at in range(INNER):
        copies = []
        here = pl.ds(at * tile, tile)
        for side in range(sides):
            columns = pl.ds(side * half, half)
            for i, target in enumerate((gate_w, up_w)):
                source = weights[side][i].at[0, pl.ds(depth + at * tile, tile)]
                copies.append(
                    fetch(source, target.at[here, columns], weight_sem.at[at, 2 * side + i])
                )
        copies.append(fetch(mine.at[:, here], x.at[:, here], row_sem.at[at]))
        waits.append(copies)
    ring_waits = [
        fetch(gate_ring, gate, row_sem.at[INNER]),
        fetch(up_ring, up, row_sem.at[INNER + 1]),
    ]
    down_waits = [
        fetch(weights[side][2].at[0], down_w.at[pl.ds(side * half, half)], weight_sem.at[INNER, side])
        for side in range(sides)
    ]

    for at in range(INNER):
        for copy in waits[at]:
            copy.wait()
        here = slice(at * tile, (at + 1) * tile)
        gate_part = dot(x[:, here], gate_w[here])
        up_part = dot(x[:, here], up_w[here])
        if at == 0:
            gate_rest[...] = gate_part
            up_rest[...] = up_part
        else:
            gate_rest[...] += gate_part
            up_rest[...] += up_part
    for copy in ring_waits:
        copy.wait()
    for turn in range(planes):
        for f in range(own):
            start = (f * planes + turn) * OWNED
            target = slice(f * OWNED, (f + 1) * OWNED)
            gate[turn, target] += gate_rest[start : start + OWNED]
            up[turn, target] += up_rest[start : start + OWNED]
    gated = gate[...]
    hidden = gated * jax.nn.sigmoid(gated) * up[...]
    gate[...] = hidden
    for copy in down_waits:
        copy.wait()
    hidden = hidden.reshape(planes * block, gate.shape[2]).astype(BF16)
    sends = []
    for at in range(0, size, SLAB):
        columns = slice(at, min(at + SLAB, size))
        share_ring[:, columns] = dot(hidden, down_w[:, columns]).astype(BF16)
    for turn in range(planes):
        piece = share_ring.at[pl.ds(turn * block, block)]
        sends.append(fetch(piece, outs[turn], sent.at[turn]))
        for f in range(own):
            start = (f * planes + turn) * OWNED
            spread[start : start + OWNED] = gate[turn, f * OWNED : (f + 1) * OWNED]
    share_rest[...] = dot(spread[...].astype(BF16), down_w[:, size:]).astype(BF16)
    sends.append(fetch(share_rest, outs[planes], sent.at[planes]))
    for copy in sends:
        copy.wait()


def expert(gate_ring, up_ring, mine, weights, size):
    planes, block, hidden = gate_ring.shape
    sides = len(weights)
    count, rest = mine.shape
    width = weights[0][2].shape[2]
    wide = (planes, block, hidden)
    anywhere = pl.BlockSpec(memory_space=pl.ANY)
    return pl.pallas_call(
        lambda *refs: expert_kernel(planes, sides, *refs),
        out_shape=[jax.ShapeDtypeStruct((block, size), BF16)] * planes
        + [jax.ShapeDtypeStruct((count, width - size), BF16)],
        in_specs=[anywhere] * (3 + 3 * sides),
        out_specs=[anywhere] * (planes + 1),
        scratch_shapes=[
            pltpu.VMEM((count, rest), BF16),
            pltpu.VMEM((rest, hidden), BF16),
            pltpu.VMEM((rest, hidden), BF16),
            pltpu.VMEM((hidden, width), BF16),
            pltpu.VMEM((count, hidden), F32),
            pltpu.VMEM((count, hidden), F32),
            pltpu.VMEM(wide, F32),
            pltpu.VMEM(wide, F32),
            pltpu.VMEM((count, hidden), F32),
            pltpu.VMEM((count, size), BF16),
            pltpu.VMEM((count, width - size), BF16),
            pltpu.SemaphoreType.DMA((INNER + 2,)),
            pltpu.SemaphoreType.DMA((INNER + 1, 2 * sides)),
            pltpu.SemaphoreType.DMA((planes + 1,)),
        ],
        compiler_params=pltpu.CompilerParams(vmem_limit_bytes=63 << 20),
        cost_estimate=pl.CostEstimate(
            flops=4 * count * rest * hidden + 2 * count * width * hidden,
            bytes_accessed=2 * count * (width + rest) + (4 * rest + 2 * width) * hidden,
            transcendentals=count * hidden,
        ),
    )(gate_ring, up_ring, mine, *[v for side in weights for v in side])


def local(
    query_latent,
    query_rope,
    cache_latent,
    cache_rope,
    lengths,
    value_up,
    out_proj,
    residual,
    norm_gain,
    expert_ids,
    route_weights,
    gate_proj,
    up_proj,
    down_proj,
):
    row_count, width = residual.shape
    owners = lax.axis_size("ffn")
    cores = 2
    planes = lax.axis_size("attn") // cores
    swap = [(a, a ^ 1) for a in range(planes * cores)]

    def from_plane(v, ahead):
        pairs = [
            (((y + ahead) % planes) * cores + c, y * cores + c)
            for y in range(planes)
            for c in range(cores)
        ]
        return lax.ppermute(v, "attn", pairs)

    def along_planes(v):
        return jnp.stack([v] + [from_plane(v, ahead) for ahead in range(1, planes)])

    named = expert_ids[:, :, None] == jnp.arange(owners, dtype=jnp.int32)[None, None, :]
    routed = jnp.sum(named.astype(F32), axis=1)
    row_weights = jnp.sum(jnp.where(named, route_weights[:, :, None], F32(0.0)), axis=1)
    capacity = min(row_count, row_count * expert_ids.shape[1] // owners + 1)

    def slots_of(routed, weight):
        rank = jnp.cumsum(routed, axis=-2) - routed
        routed, weight, rank = (jnp.moveaxis(v, -1, 0)[..., None, :] for v in (routed, weight, rank))
        slot = jnp.arange(capacity, dtype=jnp.int32).astype(F32)[:, None]
        placed = ((routed == 1.0) & (rank == slot)).astype(F32)
        return placed, placed * weight

    score_scale = (value_up.shape[2] + query_rope.shape[2]) ** (-0.5)
    pieces = attend(
        query_latent,
        query_rope,
        cache_latent,
        cache_rope,
        lengths,
        value_up,
        out_proj,
        score_scale,
        owners,
        PARTS,
    )
    eye = jnp.eye(planes, dtype=F32)

    def block_diagonal(v):
        spread = v[:, :, :, None, :] * eye[None, :, None, :, None]
        return spread.reshape(owners * planes * capacity, planes * row_count)

    placed, weighting = slots_of(routed, row_weights)
    placed = placed.reshape(owners * capacity, row_count).astype(BF16)
    weighting = weighting.reshape(owners * capacity, row_count)
    terms, left = [routed], row_weights
    for _ in range(3):
        term = lax.reduce_precision(left, 8, 7)
        terms.append(term)
        left = left - term
    table = jnp.pad(jnp.concatenate(terms, axis=1), ((0, 0), (0, 128 - 4 * owners))).astype(BF16)
    pieces = lax.all_to_all(pieces, "ffn", split_axis=0, concat_axis=0, tiled=True)
    weights_here = (gate_proj, up_proj, down_proj)
    weights_there = [lax.ppermute(v, "attn", swap) for v in weights_here]
    pieces, weights_there = lax.optimization_barrier((pieces, weights_there))
    attended = (
        jnp.sum(pieces.astype(F32), axis=0)
        .reshape(PARTS, row_count, width // PARTS)
        .transpose(1, 0, 2)
        .reshape(row_count, width)
    )
    mixed = residual.astype(F32) + attended
    inverse = lax.rsqrt(jnp.mean(mixed * mixed, axis=1, keepdims=True) + 1e-06)
    normed = (mixed * inverse * norm_gain.astype(F32)[None, :]).astype(BF16)

    outgoing = dot(placed, normed[:, :IN_RING]).astype(BF16).reshape(owners, capacity, IN_RING)
    near = jnp.concatenate([normed[:, IN_RING:], table], axis=1)
    arrived = lax.all_to_all(outgoing, "ffn", split_axis=0, concat_axis=0, tiled=True)
    arrived = arrived.reshape(owners * capacity, IN_RING)

    rest = width - IN_RING
    by_plane = [arrived] + [from_plane(arrived, ahead) for ahead in range(1, planes)]
    near = along_planes(near)
    tables = near[:, :, rest:].astype(F32)
    tables = [tables[:, :, at * owners : (at + 1) * owners] for at in range(4)]
    placed_all, weighting_all = slots_of(tables[0], tables[1] + tables[2] + tables[3])
    placed_all = block_diagonal(placed_all).astype(BF16)
    weighting_all = block_diagonal(weighting_all)
    near = near[:, :, :rest].reshape(planes * row_count, rest)
    outgoing = dot(placed_all, near).astype(BF16).reshape(owners, planes * capacity, rest)
    mine = lax.all_to_all(outgoing, "ffn", split_axis=0, concat_axis=0, tiled=True)
    weights = (weights_here, weights_there)
    gate_ring, up_ring = expert_front(by_plane, weights)
    gate_ring, up_ring, mine = lax.optimization_barrier((gate_ring, up_ring, mine))
    mine = mine.reshape(owners * planes * capacity, rest)
    *ring, ours = expert(gate_ring, up_ring, mine, weights, OUT_RING)

    summed = ring[0].astype(F32)
    for ahead in range(1, planes):
        summed = summed + from_plane(ring[planes - ahead], ahead).astype(F32)
    summed = summed.astype(BF16)

    rest = width - OUT_RING
    ours = ours.reshape(owners, planes * capacity, rest)
    ours = lax.all_to_all(ours, "ffn", split_axis=0, concat_axis=0, tiled=True)
    ours = jnp.einsum(
        "sr,sd->rd",
        weighting_all,
        ours.reshape(owners * planes * capacity, rest).astype(F32),
        precision=lax.Precision.HIGHEST,
    ).astype(BF16)
    ours = ours.reshape(planes, row_count, rest)
    sum_rest = ours[0].astype(F32)
    for ahead in range(1, planes):
        sum_rest = sum_rest + from_plane(ours[planes - ahead], ahead).astype(F32)

    returned = lax.all_to_all(
        summed.reshape(owners, capacity, OUT_RING), "ffn", split_axis=0, concat_axis=0, tiled=True
    )
    sum_ring = jnp.einsum(
        "sr,sd->rd",
        weighting,
        returned.reshape(owners * capacity, OUT_RING).astype(F32),
        precision=lax.Precision.HIGHEST,
    )
    return (mixed + jnp.concatenate([sum_ring, sum_rest], axis=1)).astype(BF16)


def solution(mesh):
    return jax.shard_map(
        local,
        mesh=mesh,
        in_specs=(
            P("attn", "ffn", None),
            P("attn", "ffn", None),
            P("attn", None, None),
            P("attn", None, None),
            P("attn"),
            P("ffn", None, None),
            P("ffn", None, None),
            P(("attn", "ffn"), None),
            P(),
            P(("attn", "ffn"), None),
            P(("attn", "ffn"), None),
            P("ffn", None, "attn"),
            P("ffn", None, "attn"),
            P("ffn", "attn", None),
        ),
        out_specs=P(("attn", "ffn"), None),
        check_vma=False,
    )
```
